32 devices in a mesh: shot: 4 (over z), bin: 8 (over y, x, core).
Axes of the slice: x: 2, y: 2, z: 4, core: 2. Of those that a mesh axis runs over, the one named last changes fastest.
Arguments:
- traces: bfloat16 [8192, 2048], P(('shot', 'bin')), may hold values from -6 to 6
- shot_filter: bfloat16 [32, 128], P(('shot', 'bin')), may hold values from -0.5 to 0.5
- channel_gain: float32 [256], replicated, may hold values from 0.5 to 2
- bin_owner: int32 [8192, 1], P(('shot', 'bin')), may hold values from 0 to 31; in each aligned block of 256 rows (0 to 255, 256 to 511, ...) at most 16 rows name the same one
- bin_slot: int32 [8192], P(('shot', 'bin')), may hold values from 0 to 15
- offset_class: int32 [8192], P(('shot', 'bin')), may hold values from 0 to 31
- dip_filter: bfloat16 [9, 31], replicated, may hold values from -0.375 to 0.375
- nmo_start: int32 [32, 2048], replicated, may hold values from 0 to 2040, as said below
- nmo_weights: bfloat16 [32, 8, 2048], replicated, may hold values from -2.09375 to 2.09375
Outputs:
- stacked: float32 [8, 64, 2048], P('shot', 'bin')
The draws below stay inside these ranges and needn't reach their ends.
Inputs may be any that keep to these rules, and one draw needn't show every extreme that they name: `bin_owner`: among the rows of one device, at most 16 name any one block. `nmo_start`: band starts leave room for all 8 taps and lie at most 64 samples before their output sample.
All inputs are finite; a program needn't handle non-finite values.
Results may differ from the reference program's by a relative error of at most 0.0042.
Values may be sent and summed in bfloat16 or wider, within the bound.
A program may use at most 256 MiB of HBM per device.

```python
import math
import jax
import jax.numpy as jnp
import numpy as np
from jax import lax

NT = 2048
DECON_TAPS = 128
DIP_XL = 9
DIP_T = 31
NMO_TAPS = 8
NOFF = 32
CHANNELS = 256
IL_DEV = 2
XL_DEV = 8
OWNERS = 32
TR_DEV = 256
TRACES = 8192
SHOTS = 32
CAP = 16
BINS_DEV = 16
NIL = 8
NXL = 64
N_BIN = 8


def draw_nmo_start(key, part):
    delays = jax.random.randint(key, (NOFF, NT), 0, 64)
    sample_times = jnp.arange(NT, dtype=jnp.int32)[None, :]
    return jnp.clip(sample_times + delays - 64, 0, NT - NMO_TAPS).astype(jnp.int32)


def plant(result, stream_key, low, largest):
    dims = result.shape
    index_at = [jax.random.randint(jax.random.fold_in(stream_key, axis), (), 0, dims[axis]) for axis in range(len(dims))]
    result = result.at[tuple(index_at)].set(low)
    longest = dims.index(max(dims))
    index_at[longest] = (index_at[longest] + 1) % dims[longest]
    return result.at[tuple(index_at)].set(largest)


def level_of(own_key, extent, pieces, smallest, high):
    def one(axis_at, parts):
        heights = jax.random.uniform(jax.random.fold_in(jax.random.fold_in(own_key, 6), axis_at), (parts,), jnp.float32, smallest / len(pieces), high / len(pieces))
        return jnp.repeat(jnp.exp(heights), extent[axis_at] // parts).reshape((-1,) + (1,) * (len(extent) - axis_at - 1))

    level = one(*pieces[0])
    for cut in pieces[1:]:
        level = level * one(*cut)
    return level


def deal_out(own_key, own, number, rows, number_of, top, most, lean):
    ranking = jax.random.permutation(own_key, number_of)
    crowded, common = shares(number_of, rows * top, most, lean, True), shares(number_of, rows * top, most, lean, False)
    places = jnp.arange(number_of)

    def named(sizes, offset_by):
        used = int((sizes > 0).sum())
        fixed = max(1, used // 4)
        shifted = fixed + (places - fixed + offset_by * (used - fixed)) % max(1, number_of - fixed)
        return jnp.zeros((number_of,), jnp.int32).at[ranking[jnp.where(places < fixed, places, shifted)]].set(jnp.asarray(sizes, jnp.int32))

    sizes = jnp.where(number % 4 == 0, named(crowded, number // 4), named(common, number - number // 4 - 1))
    mixed = jax.random.permutation(jax.random.fold_in(own, 3), number_of)
    donor, sink = mixed[0:number_of // 2 * 2:2], mixed[1:number_of // 2 * 2:2]
    slack = jnp.minimum(sizes[donor] - 1, most - sizes[sink]) // 2
    slack = jnp.where((donor == ranking[0]) | (sink == ranking[0]) | (sizes[sink] == 0), 0, jnp.maximum(slack, 0))
    shifted = jax.random.randint(jax.random.fold_in(own, 4), (number_of // 2,), 0, 1 << 20) % (slack + 1)
    sizes = sizes.at[donor].add(-shifted).at[sink].add(shifted)
    items = jnp.searchsorted(jnp.cumsum(sizes), jnp.arange(rows * top), side="right").astype(jnp.int32)
    listing = items.reshape(top, rows).T
    listing = listing[jax.random.permutation(jax.random.fold_in(own, 1), rows)]
    offset_by = jax.random.randint(jax.random.fold_in(own, 2), (rows, 1), 0, top)
    return jnp.take_along_axis(listing, (jnp.arange(top)[None, :] + offset_by) % top, axis=1)


def shares(count, total, reach, slope, full):
    loads = [(1 << 20) // math.isqrt(standing ** slope) + 1 for standing in range(1, count + 1)]
    largest = reach if full else min(reach, max(-(-total // count), total * loads[0] // sum(loads)))
    least = 1 if total - largest >= count - 1 else 0
    holding, rest = [largest] + [least] * (count - 1), total - largest - least * (count - 1)
    while rest > 0:
        candidates = [i for i in range(1, count) if holding[i] < largest] or [i for i in range(1, count) if holding[i] < reach]
        mass, remaining = sum([loads[i] for i in candidates]), rest
        for i in candidates:
            addition = min(reach - holding[i], max(1, remaining * loads[i] // mass), rest)
            holding[i] = holding[i] + addition
            rest = rest - addition
    return np.array(holding)


def scatter_about(rng, extent, deviation, reach, cuts=(), held_as=jnp.bfloat16):
    array = deviation * jax.random.normal(rng, extent, jnp.float32)
    if cuts:
        array = array * level_of(rng, extent, cuts, -0.22, 0.18)
    return jnp.clip(array, -reach, reach).astype(held_as)


def setup_inputs(seed: int = 0) -> dict:
    keys = jax.random.split(jax.random.key(seed), 10)
    traces = scatter_about(keys[0], (TRACES, NT), 1.0, 6.0, ((0, 32),))
    shot_filter = scatter_about(keys[1], (SHOTS, DECON_TAPS), DECON_TAPS ** -0.5, 0.5, ((0, 32),))
    channel_gain = jnp.clip(jnp.exp(jax.random.uniform(keys[2], (CHANNELS,), jnp.float32, math.log(0.5), math.log(2.0))), 0.5, 2.0)
    bin_owner_keys = jax.random.split(jax.random.fold_in(keys[3], 1), TRACES // TR_DEV)
    bin_owner_turns = jax.random.permutation(jax.random.fold_in(keys[3], 3), TRACES // TR_DEV)
    bin_owner = jax.vmap(lambda own, number: deal_out(jax.random.fold_in(keys[3], 2), own, number, TR_DEV, OWNERS, 1, CAP, 2))(bin_owner_keys, bin_owner_turns).reshape((TRACES, 1))
    bin_slot = plant(jax.random.randint(keys[4], (TRACES,), 0, BINS_DEV), jax.random.fold_in(keys[4], 1), 0, BINS_DEV - 1).astype(jnp.int32)
    offset_class = plant(jax.random.randint(keys[5], (TRACES,), 0, NOFF), jax.random.fold_in(keys[5], 1), 0, NOFF - 1).astype(jnp.int32)
    dip_filter = scatter_about(keys[6], (DIP_XL, DIP_T), (DIP_XL * DIP_T) ** -0.5, 0.375)
    nmo_start = draw_nmo_start(jax.random.fold_in(keys[9], 71), 0)
    nmo_weights = scatter_about(keys[8], (NOFF, NMO_TAPS, NT), 0.35, 2.09375)
    return {"traces": traces, "shot_filter": shot_filter, "channel_gain": channel_gain, "bin_owner": bin_owner, "bin_slot": bin_slot, "offset_class": offset_class, "dip_filter": dip_filter, "nmo_start": nmo_start, "nmo_weights": nmo_weights}


def later_block(values):
    pad_zero = jnp.zeros_like(values[..., :1, :])
    return jnp.concatenate((pad_zero, values[..., :-1, :]), axis=-2)

def earlier_block(values):
    pad_zero = jnp.zeros_like(values[..., :1, :])
    return jnp.concatenate((values[..., 1:, :], pad_zero), axis=-2)

def decon_matrices_of(shot_filter):
    row_index = jnp.arange(128, dtype=jnp.int32)[:, None]
    col_index = jnp.arange(256, dtype=jnp.int32)[None, :]
    lag_index = col_index % 128 - row_index - 128 * (col_index // 128 - 1)
    valid = (lag_index >= 0) & (lag_index < 128)
    picked = jnp.take(shot_filter, jnp.clip(lag_index, 0, 127).reshape(-1), axis=1).reshape(shot_filter.shape[0], 128, 256)
    return jnp.where(valid[None], picked, jnp.zeros((), shot_filter.dtype)).astype(jnp.bfloat16)

def dip_matrices_of(dip_filter):
    time_taps = dip_filter.shape[1]
    row_index = jnp.arange(128, dtype=jnp.int32)[:, None]
    col_index = jnp.arange(384, dtype=jnp.int32)[None, :]
    difference = 128 * (col_index // 128 - 1) + row_index - col_index % 128 + time_taps // 2
    valid = (difference >= 0) & (difference < time_taps)
    picked = jnp.take(dip_filter, jnp.clip(difference, 0, time_taps - 1).reshape(-1), axis=1).reshape(dip_filter.shape[0], 128, 384)
    return jnp.where(valid[None], picked, jnp.zeros((), dip_filter.dtype)).astype(jnp.bfloat16)

def dip_sum(padded, matrices, out_width):
    lead = padded.shape[0]
    offsets = padded.shape[2]
    blocks = padded.shape[3] // 128
    block_shape = (lead, out_width, offsets, blocks, 128)
    summed = jnp.zeros(block_shape, jnp.float32)
    for tap_index in range(matrices.shape[0]):
        trace_rows = padded[:, tap_index:tap_index + out_width].reshape(-1, 128)
        before = jnp.dot(trace_rows, matrices[tap_index, :, :128], preferred_element_type=jnp.float32).reshape(block_shape)
        centre = jnp.dot(trace_rows, matrices[tap_index, :, 128:256], preferred_element_type=jnp.float32).reshape(block_shape)
        following = jnp.dot(trace_rows, matrices[tap_index, :, 256:], preferred_element_type=jnp.float32).reshape(block_shape)
        summed = summed + later_block(before) + centre + earlier_block(following)
    return summed

def move_out(filtered, band_start, weights):
    summed = jnp.zeros(filtered.shape, jnp.float32)
    for tap_index in range(weights.shape[1]):
        sample_index = jnp.broadcast_to((band_start + tap_index)[None], filtered.shape)
        picked = jnp.take_along_axis(filtered, sample_index, axis=2).astype(jnp.float32)
        summed = summed + picked * weights[:, tap_index, :].astype(jnp.float32)[None]
    return lax.optimization_barrier(jnp.sum(summed, axis=1)) / math.sqrt(filtered.shape[1])

def reference(traces, shot_filter, channel_gain, bin_owner, bin_slot, offset_class, dip_filter, nmo_start, nmo_weights):
    blocks = NT // 128
    decon_matrices = decon_matrices_of(shot_filter)
    shot_rows = traces.reshape(SHOTS, CHANNELS * blocks, 128)

    def apply_shot(shot_pair):
        trace_rows, matrix = shot_pair
        product = jnp.dot(trace_rows, matrix, preferred_element_type=jnp.float32).reshape(CHANNELS, blocks, 256)
        return later_block(product[:, :, :128]) + product[:, :, 128:]
    convolved = lax.map(apply_shot, (shot_rows, decon_matrices))
    deconvolved = (convolved * channel_gain[None, :, None, None]).astype(jnp.bfloat16).reshape(TRACES, NT)
    owner_index = bin_owner[:, 0]
    inline = owner_index // N_BIN * IL_DEV + bin_slot // XL_DEV
    crossline = owner_index % N_BIN * XL_DEV + bin_slot % XL_DEV
    cell = ((inline * NXL + crossline) * NOFF + offset_class).astype(jnp.int32)
    cell_total = NIL * NXL * NOFF
    summed = jax.ops.segment_sum(deconvolved.astype(jnp.float32), cell, num_segments=cell_total)
    fold_count = jax.ops.segment_sum(jnp.ones((TRACES,), jnp.float32), cell, num_segments=cell_total)
    binned = (summed / jnp.maximum(fold_count, 1.0)[:, None]).astype(jnp.bfloat16).reshape(NIL, NXL, NOFF, NT)
    dip_matrices = dip_matrices_of(dip_filter)
    rim_width = DIP_XL // 2
    padded = jnp.pad(binned, ((0, 0), (rim_width, rim_width), (0, 0), (0, 0)))

    def apply_inline(inline_plane):
        summed_dip = dip_sum(inline_plane[None], dip_matrices, NXL)[0]
        filtered = summed_dip.reshape(NXL, NOFF, NT).astype(jnp.bfloat16)
        return move_out(filtered, nmo_start, nmo_weights)
    return lax.map(apply_inline, padded)
```

```python
import functools
import math

import jax
import jax.numpy as jnp
from jax import lax
from jax.experimental import pallas as pl
from jax.experimental.pallas import tpu as pltpu
from jax.sharding import PartitionSpec as P

IL_DEV = 2
XL_DEV = 8
MESH = pl.DeviceIdType.MESH
AXES = ("shot", "bin")
VMEM_BYTES = 40 * 1024 * 1024


def iota(shape, dim):
    return lax.broadcasted_iota(jnp.int32, shape, dim)


def toeplitz(row):
    return pltpu.roll(jnp.broadcast_to(row, (256, 256)), 0, 1, stride=1, stride_axis=0)


def decon_kernel(owners, capacity, traces, filters, gain, owner_row, out, dec):
    trace_count, samples = traces.shape
    shots = filters.shape[0]
    channels = gain.shape[0]
    for shot in range(shots):
        taps = filters[shot : shot + 1, :].astype(jnp.float32)
        matrix = toeplitz(jnp.concatenate([jnp.zeros_like(taps), taps], axis=1))[:, :128]
        matrix = matrix.astype(jnp.bfloat16)
        rows = slice(shot * channels, (shot + 1) * channels)
        for block in range(samples // 128):
            lanes = slice(128 * block, 128 * block + 128)
            if block == 0:
                product = jnp.dot(
                    traces[rows, lanes], matrix[128:], preferred_element_type=jnp.float32
                )
            else:
                window = slice(128 * block - 128, 128 * block + 128)
                product = jnp.dot(
                    traces[rows, window], matrix, preferred_element_type=jnp.float32
                )
            dec[rows, lanes] = (product * gain[...]).astype(jnp.bfloat16)
    hit = iota((owners, trace_count), 0) == owner_row[...]
    hit_f = jnp.where(hit, 1.0, 0.0)
    upper = iota((trace_count, trace_count), 0) <= iota((trace_count, trace_count), 1)
    running = jnp.dot(
        hit_f.astype(jnp.bfloat16),
        jnp.where(upper, 1.0, 0.0).astype(jnp.bfloat16),
        preferred_element_type=jnp.float32,
    )
    rank = jnp.sum(jnp.where(hit, running - 1.0, 0.0), axis=0, keepdims=True)
    position = owner_row[...] * capacity + rank.astype(jnp.int32)
    slots = owners * capacity
    pick = jnp.where(iota((slots, trace_count), 0) == position, 1.0, 0.0).astype(jnp.bfloat16)
    for lane in range(0, samples, 256):
        out[:, lane : lane + 256] = jnp.dot(
            pick, dec[:, lane : lane + 256], preferred_element_type=jnp.float32
        ).astype(jnp.bfloat16)


def exchange_kernel(shots, bins, out_ref, in_ref, send_sem, recv_sem, own_sem):
    count = shots * bins
    me = lax.axis_index("shot") * bins + lax.axis_index("bin")
    barrier = pltpu.get_barrier_semaphore()

    def greet(step, carry):
        other = lax.rem(me + step, count)
        pl.semaphore_signal(
            barrier, inc=1, device_id=(other // bins, lax.rem(other, bins)), device_id_type=MESH
        )
        return carry

    lax.fori_loop(1, count, greet, 0)
    own = pltpu.make_async_copy(out_ref.at[me], in_ref.at[me], own_sem)
    own.start()
    pl.semaphore_wait(barrier, count - 1)

    def copy_of(step):
        other = lax.rem(me + step, count)
        return pltpu.make_async_remote_copy(
            src_ref=out_ref.at[other],
            dst_ref=in_ref.at[me],
            send_sem=send_sem.at[step],
            recv_sem=recv_sem.at[step],
            device_id=(other // bins, lax.rem(other, bins)),
            device_id_type=MESH,
        )

    def begin(step, carry):
        copy_of(step).start()
        return carry

    def finish(step, carry):
        copy_of(step).wait()
        return carry

    lax.fori_loop(1, count, begin, 0)
    own.wait()
    lax.fori_loop(1, count, finish, 0)


def exchange(outgoing, collective_id):
    shots, bins = lax.axis_size("shot"), lax.axis_size("bin")
    count = shots * bins
    return pl.pallas_call(
        functools.partial(exchange_kernel, shots, bins),
        out_shape=jax.ShapeDtypeStruct(outgoing.shape, outgoing.dtype),
        in_specs=[pl.BlockSpec(memory_space=pl.ANY)],
        out_specs=pl.BlockSpec(memory_space=pl.ANY),
        scratch_shapes=[
            pltpu.SemaphoreType.DMA((count,)),
            pltpu.SemaphoreType.DMA((count,)),
            pltpu.SemaphoreType.DMA,
        ],
        compiler_params=pltpu.CompilerParams(
            collective_id=collective_id, has_side_effects=True
        ),
        name="exchange",
    )(outgoing)


def bin_kernel(capacity, cells_here, arrived, codes, lo, hi):
    owners, trace_count = codes.shape
    slots, samples = arrived.shape
    local = codes[...]
    mine = (local >= 0) & (local < cells_here)
    upper = iota((trace_count, trace_count), 0) <= iota((trace_count, trace_count), 1)
    running = jnp.dot(
        jnp.where(mine, 1.0, 0.0).astype(jnp.bfloat16),
        jnp.where(upper, 1.0, 0.0).astype(jnp.bfloat16),
        preferred_element_type=jnp.float32,
    )
    ranked = jnp.where(mine, running, 0.0)
    named = local.astype(jnp.float32) + 1.0
    place = iota((owners, slots), 1) - capacity * iota((owners, slots), 0)
    spread = jnp.zeros((owners, slots), jnp.float32)
    for rank in range(capacity):
        code = jnp.sum(jnp.where(ranked == rank + 1.0, named, 0.0), axis=1, keepdims=True)
        spread = jnp.where(place == rank, code, spread)
    slot_code = jnp.sum(spread, axis=0, keepdims=True).astype(jnp.int32)
    member_f = jnp.where(iota((cells_here, slots), 0) + 1 == slot_code, 1.0, 0.0)
    fold = jnp.sum(member_f, axis=1, keepdims=True)
    scale = 1.0 / jnp.maximum(fold, 1.0)
    member = member_f.astype(jnp.bfloat16)
    offsets = lo.shape[2]
    half = XL_DEV // 2
    for lane in range(0, samples, 256):
        summed = jnp.dot(
            member, arrived[:, lane : lane + 256], preferred_element_type=jnp.float32
        )
        binned = (summed * scale).astype(jnp.bfloat16).reshape(IL_DEV, XL_DEV, offsets, 256)
        lo[:, :, :, lane : lane + 256] = binned[:, :half]
        hi[:, :, :, lane : lane + 256] = binned[:, half:]


def stack_kernel(
    taps, left, lo, hi, right, dip_rows, start, weights, out, ext, matrix, filtered, sems
):
    crosslines = ext.shape[1]
    offsets = ext.shape[2]
    samples = ext.shape[3] - 256
    blocks = samples // 128
    half = crosslines // 4
    copies = []
    for part, ref in enumerate((left, lo, hi, right)):
        copy = pltpu.make_async_copy(
            ref,
            ext.at[:, part * half : part * half + half, :, 128 : 128 + samples],
            sems.at[part],
        )
        copy.start()
        copies.append(copy)
    zero = jnp.zeros((IL_DEV, crosslines, offsets, 128), jnp.bfloat16)
    ext[:, :, :, :128] = zero
    ext[:, :, :, 128 + samples :] = zero
    matrix[...] = jnp.zeros(matrix.shape, jnp.bfloat16)
    for tap in range(taps):
        one = toeplitz(dip_rows[tap : tap + 1, :])[:, :128].astype(jnp.bfloat16)
        matrix[256 * tap : 256 * tap + 256, :128] = one
        matrix[256 * tap + 256 : 256 * tap + 512, 128:] = one
    for copy in copies:
        copy.wait()
    pairs = XL_DEV // 2

    def filter_block(block, carry):
        lanes = pl.ds(pl.multiple_of(128 * block, 128), 256)
        window = ext[:, :, :, lanes].reshape(IL_DEV, crosslines // 2, 2, offsets, 256)
        pieces = []
        for tap in range(taps + 1):
            piece = window[:, tap // 2 : tap // 2 + pairs, tap % 2]
            pieces.append(piece.reshape(IL_DEV * pairs * offsets, 256))
        result = jnp.dot(
            jnp.concatenate(pieces, axis=1), matrix[...], preferred_element_type=jnp.float32
        )
        rounded = result.astype(jnp.bfloat16).astype(jnp.float32)
        for side in range(2):
            filtered[block, :, :, side] = rounded[:, 128 * side : 128 * side + 128].reshape(
                IL_DEV, pairs, offsets, 128
            )
        return carry

    lax.fori_loop(0, blocks + 1, filter_block, 0)
    nmo_taps = weights.shape[0]
    scale = 1.0 / math.sqrt(offsets)

    def stack_block(block, carry):
        lanes = pl.ds(pl.multiple_of(128 * block, 128), 128)
        totals = [jnp.zeros((8, 128), jnp.float32) for _ in range(IL_DEV * XL_DEV)]
        for first in range(0, offsets, 8):
            group = slice(first, first + 8)
            at = start[group, lanes] - (128 * block - 64)
            index, early, weight = [], [], []
            for tap in range(nmo_taps):
                moved = at + tap
                index.append(moved & 127)
                early.append(moved < 128)
                weight.append(weights[tap, group, lanes])
            for cell in range(IL_DEV * XL_DEV):
                place = (cell // XL_DEV, cell % XL_DEV // 2, cell % 2)
                here = filtered[(block,) + place + (group, slice(None))]
                after = filtered[(block + 1,) + place + (group, slice(None))]
                for tap in range(nmo_taps):
                    value = jnp.where(
                        early[tap],
                        jnp.take_along_axis(here, index[tap], axis=1),
                        jnp.take_along_axis(after, index[tap], axis=1),
                    )
                    totals[cell] = totals[cell] + value * weight[tap]
        for inline in range(IL_DEV):
            rows = [
                jnp.sum(totals[inline * XL_DEV + x], axis=0, keepdims=True) for x in range(XL_DEV)
            ]
            out[inline, :, lanes] = jnp.concatenate(rows, axis=0) * scale
        return carry

    lax.fori_loop(0, blocks, stack_block, 0)


def per_device(
    traces,
    shot_filter,
    channel_gain,
    bin_owner,
    bin_slot,
    offset_class,
    dip_filter,
    nmo_start,
    nmo_weights,
):
    bins = lax.axis_size("bin")
    owners = lax.axis_size("shot") * bins
    me = lax.axis_index("shot") * bins + lax.axis_index("bin")
    trace_count, samples = traces.shape
    capacity = 2 * trace_count // owners
    slots = owners * capacity
    offsets = nmo_start.shape[0]
    cells_here = IL_DEV * XL_DEV * offsets
    half = XL_DEV // 2
    vmem = pl.BlockSpec(memory_space=pltpu.VMEM)
    anywhere = pl.BlockSpec(memory_space=pl.ANY)
    params = pltpu.CompilerParams(vmem_limit_bytes=VMEM_BYTES)

    owner = bin_owner[:, 0]
    code = owner * cells_here + bin_slot * offsets + offset_class
    codes = lax.all_gather(code, AXES) - me * cells_here

    outgoing = pl.pallas_call(
        functools.partial(decon_kernel, owners, capacity),
        out_shape=jax.ShapeDtypeStruct((slots, samples), jnp.bfloat16),
        in_specs=[vmem] * 4,
        out_specs=vmem,
        scratch_shapes=[pltpu.VMEM((trace_count, samples), jnp.bfloat16)],
        compiler_params=params,
        name="decon",
    )(traces, shot_filter, channel_gain[:, None], owner[None, :])

    arrived = exchange(outgoing.reshape(owners, capacity, samples), 1)

    rim = jax.ShapeDtypeStruct((IL_DEV, half, offsets, samples), jnp.bfloat16)
    lo, hi = pl.pallas_call(
        functools.partial(bin_kernel, capacity, cells_here),
        out_shape=(rim, rim),
        in_specs=[vmem] * 2,
        out_specs=(vmem, vmem),
        compiler_params=params,
        name="bin",
    )(arrived.reshape(slots, samples), codes)

    right = lax.ppermute(lo, "bin", [(i + 1, i) for i in range(bins - 1)])
    left = lax.ppermute(hi, "bin", [(i, i + 1) for i in range(bins - 1)])

    taps, time_taps = dip_filter.shape
    before = 192 + time_taps // 2 - (time_taps - 1)
    dip_rows = jnp.pad(
        dip_filter[:, ::-1].astype(jnp.float32),
        ((0, 0), (before, 256 - before - time_taps)),
    )
    weights = jnp.transpose(nmo_weights, (1, 0, 2)).astype(jnp.float32)
    crosslines = 2 * XL_DEV
    return pl.pallas_call(
        functools.partial(stack_kernel, taps),
        out_shape=jax.ShapeDtypeStruct((IL_DEV, XL_DEV, samples), jnp.float32),
        in_specs=[anywhere] * 4 + [vmem] * 3,
        out_specs=vmem,
        scratch_shapes=[
            pltpu.VMEM((IL_DEV, crosslines, offsets, samples + 256), jnp.bfloat16),
            pltpu.VMEM(((taps + 1) * 256, 256), jnp.bfloat16),
            pltpu.VMEM(
                (samples // 128 + 1, IL_DEV, XL_DEV // 2, 2, offsets, 128), jnp.float32
            ),
            pltpu.SemaphoreType.DMA((4,)),
        ],
        compiler_params=params,
        name="stack",
    )(left, lo, hi, right, dip_rows, nmo_start, weights)


def solution(mesh):
    placed = (
        P(AXES, None),
        P(AXES, None),
        P(),
        P(AXES, None),
        P(AXES),
        P(AXES),
        P(),
        P(),
        P(),
    )
    return jax.shard_map(
        per_device, mesh=mesh, in_specs=placed, out_specs=P("shot", "bin", None), check_vma=False
    )
```

```python
import functools
import math

import jax
import jax.numpy as jnp
from jax import lax
from jax.experimental import pallas as pl
from jax.experimental.pallas import tpu as pltpu
from jax.sharding import PartitionSpec as P

IL_DEV = 2
XL_DEV = 8
MESH = pl.DeviceIdType.MESH
AXES = ("shot", "bin")
VMEM_BYTES = 40 * 1024 * 1024


def iota(shape, dim):
    return lax.broadcasted_iota(jnp.int32, shape, dim)


def toeplitz(row):
    return pltpu.roll(jnp.broadcast_to(row, (256, 256)), 0, 1, stride=1, stride_axis=0)


def decon_kernel(
    owners, capacity, offsets, traces, filters, gain, owner_row, slot_row, class_row, out, codes, dec
):
    trace_count, samples = traces.shape
    shots = filters.shape[0]
    channels = gain.shape[0]
    for shot in range(shots):
        taps = filters[shot : shot + 1, :].astype(jnp.float32)
        matrix = toeplitz(jnp.concatenate([jnp.zeros_like(taps), taps], axis=1))[:, :128]
        matrix = matrix.astype(jnp.bfloat16)
        rows = slice(shot * channels, (shot + 1) * channels)
        for block in range(samples // 128):
            lanes = slice(128 * block, 128 * block + 128)
            if block == 0:
                product = jnp.dot(
                    traces[rows, lanes], matrix[128:], preferred_element_type=jnp.float32
                )
            else:
                window = slice(128 * block - 128, 128 * block + 128)
                product = jnp.dot(
                    traces[rows, window], matrix, preferred_element_type=jnp.float32
                )
            dec[rows, lanes] = (product * gain[...]).astype(jnp.bfloat16)
    hit = iota((owners, trace_count), 0) == owner_row[...]
    hit_f = jnp.where(hit, 1.0, 0.0)
    upper = iota((trace_count, trace_count), 0) <= iota((trace_count, trace_count), 1)
    running = jnp.dot(
        hit_f.astype(jnp.bfloat16),
        jnp.where(upper, 1.0, 0.0).astype(jnp.bfloat16),
        preferred_element_type=jnp.float32,
    )
    rank = jnp.sum(jnp.where(hit, running - 1.0, 0.0), axis=0, keepdims=True)
    position = owner_row[...] * capacity + rank.astype(jnp.int32)
    ranked = jnp.where(iota((128, trace_count), 0) == rank.astype(jnp.int32), 1.0, 0.0)
    ranked = ranked.astype(jnp.bfloat16)

    def listed(row):
        named = jnp.where(hit, row.astype(jnp.float32), 0.0).astype(jnp.bfloat16)
        return lax.dot_general(
            named, ranked, (((1,), (1,)), ((), ())), preferred_element_type=jnp.float32
        )

    bin_part = listed(slot_row[...] + 1)
    codes[:, 0, :] = jnp.where(
        bin_part > 0, (bin_part - 1) * offsets + listed(class_row[...]) + 1, 0.0
    )
    slots = owners * capacity
    pick = jnp.where(iota((slots, trace_count), 0) == position, 1.0, 0.0).astype(jnp.bfloat16)
    for lane in range(0, samples, 256):
        out[:, lane : lane + 256] = jnp.dot(
            pick, dec[:, lane : lane + 256], preferred_element_type=jnp.float32
        ).astype(jnp.bfloat16)


def exchange_kernel(
    shots, bins, out_ref, code_out, in_ref, code_in, send_sem, recv_sem, code_send, code_recv, own_sem
):
    count = shots * bins
    me = lax.axis_index("shot") * bins + lax.axis_index("bin")
    barrier = pltpu.get_barrier_semaphore()

    def greet(step, carry):
        other = lax.rem(me + step, count)
        pl.semaphore_signal(
            barrier, inc=1, device_id=(other // bins, lax.rem(other, bins)), device_id_type=MESH
        )
        return carry

    lax.fori_loop(1, count, greet, 0)
    own = pltpu.make_async_copy(out_ref.at[me], in_ref.at[me], own_sem.at[0])
    own.start()
    own_code = pltpu.make_async_copy(code_out.at[me], code_in.at[me], own_sem.at[1])
    own_code.start()
    pl.semaphore_wait(barrier, count - 1)

    def copies_of(step):
        other = lax.rem(me + step, count)
        target = (other // bins, lax.rem(other, bins))
        rows = pltpu.make_async_remote_copy(
            src_ref=out_ref.at[other],
            dst_ref=in_ref.at[me],
            send_sem=send_sem.at[step],
            recv_sem=recv_sem.at[step],
            device_id=target,
            device_id_type=MESH,
        )
        names = pltpu.make_async_remote_copy(
            src_ref=code_out.at[other],
            dst_ref=code_in.at[me],
            send_sem=code_send.at[step],
            recv_sem=code_recv.at[step],
            device_id=target,
            device_id_type=MESH,
        )
        return rows, names

    def begin(step, carry):
        for copy in copies_of(step):
            copy.start()
        return carry

    def finish(step, carry):
        for copy in copies_of(step):
            copy.wait()
        return carry

    lax.fori_loop(1, count, begin, 0)
    own.wait()
    own_code.wait()
    lax.fori_loop(1, count, finish, 0)


def exchange(outgoing, codes, collective_id):
    shots, bins = lax.axis_size("shot"), lax.axis_size("bin")
    count = shots * bins
    return pl.pallas_call(
        functools.partial(exchange_kernel, shots, bins),
        out_shape=(
            jax.ShapeDtypeStruct(outgoing.shape, outgoing.dtype),
            jax.ShapeDtypeStruct(codes.shape, codes.dtype),
        ),
        in_specs=[pl.BlockSpec(memory_space=pltpu.VMEM)] * 2,
        out_specs=[pl.BlockSpec(memory_space=pltpu.VMEM)] * 2,
        scratch_shapes=[pltpu.SemaphoreType.DMA((count,)) for _ in range(4)]
        + [pltpu.SemaphoreType.DMA((2,))],
        compiler_params=pltpu.CompilerParams(
            collective_id=collective_id, has_side_effects=True, vmem_limit_bytes=VMEM_BYTES
        ),
        name="exchange",
    )(outgoing, codes)


def bin_kernel(capacity, cells_here, arrived, codes, lo, hi):
    owners = codes.shape[0]
    slots, samples = arrived.shape
    listed = codes[:, 0, :]
    place = iota((owners, slots), 1) - capacity * iota((owners, slots), 0)
    spread = jnp.zeros((owners, slots), jnp.float32)
    for rank in range(capacity):
        spread = jnp.where(place == rank, listed[:, rank : rank + 1], spread)
    slot_code = jnp.sum(spread, axis=0, keepdims=True).astype(jnp.int32)
    member_f = jnp.where(iota((cells_here, slots), 0) + 1 == slot_code, 1.0, 0.0)
    fold = jnp.sum(member_f, axis=1, keepdims=True)
    scale = 1.0 / jnp.maximum(fold, 1.0)
    member = member_f.astype(jnp.bfloat16)
    offsets = lo.shape[2]
    half = XL_DEV // 2
    for lane in range(0, samples, 256):
        summed = jnp.dot(
            member, arrived[:, lane : lane + 256], preferred_element_type=jnp.float32
        )
        binned = (summed * scale).astype(jnp.bfloat16).reshape(IL_DEV, XL_DEV, offsets, 256)
        lo[:, :, :, lane : lane + 256] = binned[:, :half]
        hi[:, :, :, lane : lane + 256] = binned[:, half:]


def stack_kernel(
    taps, left, lo, hi, right, dip_rows, start, weights, out, ext, matrix, filtered, sems
):
    crosslines = ext.shape[1]
    offsets = ext.shape[2]
    samples = ext.shape[3] - 256
    blocks = samples // 128
    half = crosslines // 4
    copies = []
    for part, ref in enumerate((left, lo, hi, right)):
        copy = pltpu.make_async_copy(
            ref,
            ext.at[:, part * half : part * half + half, :, 128 : 128 + samples],
            sems.at[part],
        )
        copy.start()
        copies.append(copy)
    zero = jnp.zeros((IL_DEV, crosslines, offsets, 128), jnp.bfloat16)
    ext[:, :, :, :128] = zero
    ext[:, :, :, 128 + samples :] = zero
    matrix[...] = jnp.zeros(matrix.shape, jnp.bfloat16)
    for tap in range(taps):
        one = toeplitz(dip_rows[tap : tap + 1, :])[:, :128].astype(jnp.bfloat16)
        matrix[256 * tap : 256 * tap + 256, :128] = one
        matrix[256 * tap + 256 : 256 * tap + 512, 128:] = one
    for copy in copies:
        copy.wait()
    pairs = XL_DEV // 2

    def filter_block(block, carry):
        lanes = pl.ds(pl.multiple_of(128 * block, 128), 256)
        window = ext[:, :, :, lanes].reshape(IL_DEV, crosslines // 2, 2, offsets, 256)
        pieces = []
        for tap in range(taps + 1):
            piece = window[:, tap // 2 : tap // 2 + pairs, tap % 2]
            pieces.append(piece.reshape(IL_DEV * pairs * offsets, 256))
        result = jnp.dot(
            jnp.concatenate(pieces, axis=1), matrix[...], preferred_element_type=jnp.float32
        )
        rounded = result.astype(jnp.bfloat16).astype(jnp.float32)
        for side in range(2):
            filtered[block, :, :, side] = rounded[:, 128 * side : 128 * side + 128].reshape(
                IL_DEV, pairs, offsets, 128
            )
        return carry

    lax.fori_loop(0, blocks + 1, filter_block, 0)
    nmo_taps = weights.shape[0]
    scale = 1.0 / math.sqrt(offsets)

    def stack_block(block, carry):
        lanes = pl.ds(pl.multiple_of(128 * block, 128), 128)
        totals = [jnp.zeros((8, 128), jnp.float32) for _ in range(IL_DEV * XL_DEV)]
        for first in range(0, offsets, 8):
            group = slice(first, first + 8)
            at = start[group, lanes] - (128 * block - 64)
            for tap in range(nmo_taps):
                moved = at + tap
                index = moved & 127
                early = moved < 128
                weight = weights[tap, group, lanes]
                for cell in range(IL_DEV * XL_DEV):
                    place = (cell // XL_DEV, cell % XL_DEV // 2, cell % 2)
                    here = filtered[(block,) + place + (group, slice(None))]
                    after = filtered[(block + 1,) + place + (group, slice(None))]
                    value = jnp.where(
                        early,
                        jnp.take_along_axis(here, index, axis=1),
                        jnp.take_along_axis(after, index, axis=1),
                    )
                    totals[cell] = totals[cell] + value * weight
        for inline in range(IL_DEV):
            rows = [
                jnp.sum(totals[inline * XL_DEV + x], axis=0, keepdims=True) for x in range(XL_DEV)
            ]
            out[inline, :, lanes] = jnp.concatenate(rows, axis=0) * scale
        return carry

    lax.fori_loop(0, blocks, stack_block, 0)


def per_device(
    traces,
    shot_filter,
    channel_gain,
    bin_owner,
    bin_slot,
    offset_class,
    dip_filter,
    nmo_start,
    nmo_weights,
):
    bins = lax.axis_size("bin")
    owners = lax.axis_size("shot") * bins
    trace_count, samples = traces.shape
    capacity = 2 * trace_count // owners
    slots = owners * capacity
    offsets = nmo_start.shape[0]
    cells_here = IL_DEV * XL_DEV * offsets
    half = XL_DEV // 2
    vmem = pl.BlockSpec(memory_space=pltpu.VMEM)
    anywhere = pl.BlockSpec(memory_space=pl.ANY)
    params = pltpu.CompilerParams(vmem_limit_bytes=VMEM_BYTES)

    outgoing, codes = pl.pallas_call(
        functools.partial(decon_kernel, owners, capacity, offsets),
        out_shape=(
            jax.ShapeDtypeStruct((slots, samples), jnp.bfloat16),
            jax.ShapeDtypeStruct((owners, 1, 128), jnp.float32),
        ),
        in_specs=[vmem] * 6,
        out_specs=(vmem, vmem),
        scratch_shapes=[pltpu.VMEM((trace_count, samples), jnp.bfloat16)],
        compiler_params=params,
        name="decon",
    )(
        traces,
        shot_filter,
        channel_gain[:, None],
        bin_owner.reshape(1, trace_count),
        bin_slot[None, :],
        offset_class[None, :],
    )

    arrived, codes = exchange(outgoing.reshape(owners, capacity, samples), codes, 1)

    rim = jax.ShapeDtypeStruct((IL_DEV, half, offsets, samples), jnp.bfloat16)
    lo, hi = pl.pallas_call(
        functools.partial(bin_kernel, capacity, cells_here),
        out_shape=(rim, rim),
        in_specs=[vmem] * 2,
        out_specs=(vmem, vmem),
        compiler_params=params,
        name="bin",
    )(arrived.reshape(slots, samples), codes)

    right = lax.ppermute(lo, "bin", [(i + 1, i) for i in range(bins - 1)])
    left = lax.ppermute(hi, "bin", [(i, i + 1) for i in range(bins - 1)])

    taps, time_taps = dip_filter.shape
    before = 192 + time_taps // 2 - (time_taps - 1)
    dip_rows = jnp.pad(
        dip_filter[:, ::-1].astype(jnp.float32),
        ((0, 0), (before, 256 - before - time_taps)),
    )
    weights = jnp.transpose(nmo_weights, (1, 0, 2)).astype(jnp.float32)
    crosslines = 2 * XL_DEV
    return pl.pallas_call(
        functools.partial(stack_kernel, taps),
        out_shape=jax.ShapeDtypeStruct((IL_DEV, XL_DEV, samples), jnp.float32),
        in_specs=[anywhere] * 4 + [vmem] * 3,
        out_specs=vmem,
        scratch_shapes=[
            pltpu.VMEM((IL_DEV, crosslines, offsets, samples + 256), jnp.bfloat16),
            pltpu.VMEM(((taps + 1) * 256, 256), jnp.bfloat16),
            pltpu.VMEM(
                (samples // 128 + 1, IL_DEV, XL_DEV // 2, 2, offsets, 128), jnp.float32
            ),
            pltpu.SemaphoreType.DMA((4,)),
        ],
        compiler_params=params,
        name="stack",
    )(left, lo, hi, right, dip_rows, nmo_start, weights)


def solution(mesh):
    placed = (
        P(AXES, None),
        P(AXES, None),
        P(),
        P(AXES, None),
        P(AXES),
        P(AXES),
        P(),
        P(),
        P(),
    )
    return jax.shard_map(
        per_device, mesh=mesh, in_specs=placed, out_specs=P("shot", "bin", None), check_vma=False
    )
```

```python
import functools
import math

import jax
import jax.numpy as jnp
from jax import lax
from jax.experimental import pallas as pl
from jax.experimental.pallas import tpu as pltpu
from jax.sharding import PartitionSpec as P

IL_DEV = 2
XL_DEV = 8
MESH = pl.DeviceIdType.MESH
AXES = ("shot", "bin")
VMEM_BYTES = 40 * 1024 * 1024


def iota(shape, dim):
    return lax.broadcasted_iota(jnp.int32, shape, dim)


def toeplitz(row):
    return pltpu.roll(jnp.broadcast_to(row, (256, 256)), 0, 1, stride=1, stride_axis=0)


def decon_kernel(
    owners, capacity, offsets, traces_hbm, gain_hbm, owner_hbm, slot_hbm, class_hbm, filters, *rest
):
    outs, (codes, traces, gain, owner_v, slot_v, class_v, dec, sems) = rest[:-8], rest[-8:]
    copies = [
        pltpu.make_async_copy(source, target, sems.at[number])
        for number, (source, target) in enumerate(
            (
                (owner_hbm, owner_v),
                (slot_hbm, slot_v),
                (class_hbm, class_v),
                (gain_hbm, gain),
                (traces_hbm, traces),
            )
        )
    ]
    for copy in copies:
        copy.start()
    trace_count, samples = traces.shape
    shots = filters.shape[0]
    channels = trace_count // shots
    for copy in copies[:4]:
        copy.wait()
    owner_row, slot_row, class_row = owner_v[...], slot_v[...], class_v[...]
    hit = iota((owners, trace_count), 0) == owner_row
    hit_f = jnp.where(hit, 1.0, 0.0)
    upper = iota((trace_count, trace_count), 0) <= iota((trace_count, trace_count), 1)
    running = jnp.dot(
        hit_f.astype(jnp.bfloat16),
        jnp.where(upper, 1.0, 0.0).astype(jnp.bfloat16),
        preferred_element_type=jnp.float32,
    )
    rank = jnp.sum(jnp.where(hit, running - 1.0, 0.0), axis=0, keepdims=True)
    position = owner_row * capacity + rank.astype(jnp.int32)
    ranked = jnp.where(iota((128, trace_count), 0) == rank.astype(jnp.int32), 1.0, 0.0)
    ranked = ranked.astype(jnp.bfloat16)

    def listed(row):
        named = jnp.where(hit, row.astype(jnp.float32), 0.0).astype(jnp.bfloat16)
        return lax.dot_general(
            named, ranked, (((1,), (1,)), ((), ())), preferred_element_type=jnp.float32
        )

    bin_part = listed(slot_row + 1)
    codes[:, 0, :] = jnp.where(
        bin_part > 0, (bin_part - 1) * offsets + listed(class_row) + 1, 0.0
    )
    slots = owners * capacity
    pick = jnp.where(iota((slots, trace_count), 0) == position, 1.0, 0.0).astype(jnp.bfloat16)
    factor = jnp.broadcast_to(gain[...], (128, channels)).T
    copies[4].wait()
    for shot in range(shots):
        taps = filters[shot : shot + 1, :].astype(jnp.float32)
        matrix = toeplitz(jnp.concatenate([jnp.zeros_like(taps), taps], axis=1))[:, :128]
        matrix = matrix.astype(jnp.bfloat16)
        rows = slice(shot * channels, (shot + 1) * channels)
        for block in range(samples // 128):
            lanes = slice(128 * block, 128 * block + 128)
            if block == 0:
                product = jnp.dot(
                    traces[rows, lanes], matrix[128:], preferred_element_type=jnp.float32
                )
            else:
                window = slice(128 * block - 128, 128 * block + 128)
                product = jnp.dot(
                    traces[rows, window], matrix, preferred_element_type=jnp.float32
                )
            dec[rows, lanes] = (product * factor).astype(jnp.bfloat16)
    span = samples // len(outs)
    for part, out in enumerate(outs):
        for lane in range(0, span, 256):
            place = part * span + lane
            out[:, lane : lane + 256] = jnp.dot(
                pick, dec[:, place : place + 256], preferred_element_type=jnp.float32
            ).astype(jnp.bfloat16)


def exchange_kernel(shots, bins, arrays, *refs):
    sources, targets = refs[:arrays], refs[arrays : 2 * arrays]
    send_sems = refs[2 * arrays : 3 * arrays]
    recv_sems = refs[3 * arrays : 4 * arrays]
    own_sem = refs[4 * arrays]
    count = shots * bins
    me = lax.axis_index("shot") * bins + lax.axis_index("bin")
    barrier = pltpu.get_barrier_semaphore()

    def greet(step, carry):
        other = lax.rem(me + step, count)
        pl.semaphore_signal(
            barrier, inc=1, device_id=(other // bins, lax.rem(other, bins)), device_id_type=MESH
        )
        return carry

    lax.fori_loop(1, count, greet, 0)
    own = [
        pltpu.make_async_copy(sources[k].at[me], targets[k].at[me], own_sem.at[k])
        for k in range(arrays)
    ]
    for copy in own:
        copy.start()
    pl.semaphore_wait(barrier, count - 1)

    def copies_of(step):
        other = lax.rem(me + step, count)
        return [
            pltpu.make_async_remote_copy(
                src_ref=sources[k].at[other],
                dst_ref=targets[k].at[me],
                send_sem=send_sems[k].at[step],
                recv_sem=recv_sems[k].at[step],
                device_id=(other // bins, lax.rem(other, bins)),
                device_id_type=MESH,
            )
            for k in range(arrays)
        ]

    def begin(step, carry):
        for copy in copies_of(step):
            copy.start()
        return carry

    def finish(step, carry):
        for copy in copies_of(step):
            copy.wait()
        return carry

    lax.fori_loop(1, count, begin, 0)
    for copy in own:
        copy.wait()
    lax.fori_loop(1, count, finish, 0)


def exchange(arrays, collective_id):
    shots, bins = lax.axis_size("shot"), lax.axis_size("bin")
    count = shots * bins
    number = len(arrays)
    return pl.pallas_call(
        functools.partial(exchange_kernel, shots, bins, number),
        out_shape=[jax.ShapeDtypeStruct(array.shape, array.dtype) for array in arrays],
        in_specs=[pl.BlockSpec(memory_space=pltpu.VMEM)] * number,
        out_specs=[pl.BlockSpec(memory_space=pltpu.VMEM)] * number,
        scratch_shapes=[pltpu.SemaphoreType.DMA((count,)) for _ in range(2 * number)]
        + [pltpu.SemaphoreType.DMA((number,))],
        compiler_params=pltpu.CompilerParams(
            collective_id=collective_id, has_side_effects=True, vmem_limit_bytes=VMEM_BYTES
        ),
        name=f"exchange_{collective_id}",
    )(*arrays)


def bin_kernel(capacity, cells_here, arrived, codes, lo, hi):
    owners = codes.shape[0]
    slots, samples = arrived.shape
    listed = codes[:, 0, :]
    place = iota((owners, slots), 1) - capacity * iota((owners, slots), 0)
    spread = jnp.zeros((owners, slots), jnp.float32)
    for rank in range(capacity):
        spread = jnp.where(place == rank, listed[:, rank : rank + 1], spread)
    slot_code = jnp.sum(spread, axis=0, keepdims=True).astype(jnp.int32)
    member_f = jnp.where(iota((cells_here, slots), 0) + 1 == slot_code, 1.0, 0.0)
    fold = jnp.sum(member_f, axis=1, keepdims=True)
    scale = 1.0 / jnp.maximum(fold, 1.0)
    member = member_f.astype(jnp.bfloat16)
    offsets = lo.shape[2]
    half = XL_DEV // 2
    for lane in range(0, samples, 256):
        summed = jnp.dot(
            member, arrived[:, lane : lane + 256], preferred_element_type=jnp.float32
        )
        binned = (summed * scale).astype(jnp.bfloat16).reshape(IL_DEV, XL_DEV, offsets, 256)
        lo[:, :, :, lane : lane + 256] = binned[:, :half]
        hi[:, :, :, lane : lane + 256] = binned[:, half:]


def stack_kernel(taps, first_block, halves, *refs):
    inputs = refs[: 4 * len(halves)]
    rest = refs[4 * len(halves) :]
    earlier = rest[0] if first_block else None
    dip_rows, start, weights, out, ext, matrix, ring, staged, sems = rest[1 if first_block else 0 :]
    crosslines, offsets = ext.shape[1], ext.shape[2]
    blocks = ext.shape[3] // 128 - 2
    half = crosslines // 4
    pairs = XL_DEV // 2
    copies = []
    for number, (source_lane, target_lane, span) in enumerate(halves):
        for part in range(4):
            copy = pltpu.make_async_copy(
                inputs[4 * number + part].at[:, :, :, source_lane : source_lane + span],
                ext.at[:, part * half : part * half + half, :, target_lane : target_lane + span],
                sems.at[4 * number + part],
            )
            copy.start()
            copies.append(copy)
    filled_from = min(target for _, target, _ in halves)
    filled_to = max(target + span for _, target, span in halves)
    for low, high in ((0, filled_from), (filled_to, ext.shape[3])):
        if high > low:
            ext[:, :, :, low:high] = jnp.zeros(
                (IL_DEV, crosslines, offsets, high - low), jnp.bfloat16
            )
    matrix[:256, 128:] = jnp.zeros((256, 128), jnp.bfloat16)
    matrix[256 * taps :, :128] = jnp.zeros((256, 128), jnp.bfloat16)
    for tap in range(taps):
        one = toeplitz(dip_rows[tap : tap + 1, :])[:, :128].astype(jnp.bfloat16)
        matrix[256 * tap : 256 * tap + 256, :128] = one
        matrix[256 * tap + 256 : 256 * tap + 512, 128:] = one
    if first_block:
        out[:, :, : 128 * first_block] = earlier[...]
    for copy in copies:
        copy.wait()

    def filter_block(block, target):
        lanes = pl.ds(pl.multiple_of(128 * block, 128), 256)
        window = ext[:, :, :, lanes].reshape(IL_DEV, crosslines // 2, 2, offsets, 256)
        pieces = []
        for tap in range(taps + 1):
            piece = window[:, tap // 2 : tap // 2 + pairs, tap % 2]
            pieces.append(piece.reshape(IL_DEV * pairs * offsets, 256))
        result = jnp.dot(
            jnp.concatenate(pieces, axis=1), matrix[...], preferred_element_type=jnp.float32
        )
        rounded = result.astype(jnp.bfloat16).astype(jnp.float32)
        for side in range(2):
            target[:, :, side] = rounded[:, 128 * side : 128 * side + 128].reshape(
                IL_DEV, pairs, offsets, 128
            )

    filter_block(0, ring.at[0])
    filter_block(1, ring.at[1])
    nmo_taps = weights.shape[0]
    scale = 1.0 / math.sqrt(offsets)

    def stack_block(block, carry):
        filter_block(jnp.minimum(block + 2, blocks), staged)
        this, following = lax.rem(block, 3), lax.rem(block + 1, 3)
        lanes = pl.ds(pl.multiple_of(128 * (block + first_block), 128), 128)
        totals = [jnp.zeros((8, 128), jnp.float32) for _ in range(IL_DEV * XL_DEV)]
        for first in range(0, offsets, 8):
            group = slice(first, first + 8)
            at = start[group, lanes] - (128 * (block + first_block) - 64)
            for tap in range(nmo_taps):
                moved = at + tap
                index = moved & 127
                early = moved < 128
                weight = weights[tap, group, lanes]
                for cell in range(IL_DEV * XL_DEV):
                    place = (cell // XL_DEV, cell % XL_DEV // 2, cell % 2)
                    here = ring[(this,) + place + (group, slice(None))]
                    after = ring[(following,) + place + (group, slice(None))]
                    value = jnp.where(
                        early,
                        jnp.take_along_axis(here, index, axis=1),
                        jnp.take_along_axis(after, index, axis=1),
                    )
                    totals[cell] = totals[cell] + value * weight
        for inline in range(IL_DEV):
            rows = [
                jnp.sum(totals[inline * XL_DEV + x], axis=0, keepdims=True) for x in range(XL_DEV)
            ]
            out[inline, :, lanes] = jnp.concatenate(rows, axis=0) * scale
        ring[lax.rem(block + 2, 3)] = staged[...]
        return carry

    lax.fori_loop(0, blocks, stack_block, 0)


def per_device(
    traces,
    shot_filter,
    channel_gain,
    bin_owner,
    bin_slot,
    offset_class,
    dip_filter,
    nmo_start,
    nmo_weights,
):
    bins = lax.axis_size("bin")
    owners = lax.axis_size("shot") * bins
    trace_count, samples = traces.shape
    capacity = 2 * trace_count // owners
    slots = owners * capacity
    offsets = nmo_start.shape[0]
    cells_here = IL_DEV * XL_DEV * offsets
    half = XL_DEV // 2
    vmem = pl.BlockSpec(memory_space=pltpu.VMEM)
    anywhere = pl.BlockSpec(memory_space=pl.ANY)
    params = pltpu.CompilerParams(vmem_limit_bytes=VMEM_BYTES)

    parts = 2
    span = samples // parts
    row = jax.ShapeDtypeStruct((slots, span), jnp.bfloat16)
    line = pltpu.VMEM((1, trace_count), jnp.int32)
    *outgoing, codes = pl.pallas_call(
        functools.partial(decon_kernel, owners, capacity, offsets),
        out_shape=[row] * parts + [jax.ShapeDtypeStruct((owners, 1, 128), jnp.float32)],
        in_specs=[pl.BlockSpec(memory_space=pltpu.HBM)] * 5 + [vmem],
        out_specs=[vmem] * (parts + 1),
        scratch_shapes=[
            pltpu.VMEM(traces.shape, jnp.bfloat16),
            pltpu.VMEM((1, channel_gain.shape[0]), jnp.float32),
            line,
            line,
            line,
            pltpu.VMEM(traces.shape, jnp.bfloat16),
            pltpu.SemaphoreType.DMA((5,)),
        ],
        compiler_params=params,
        name="decon",
    )(
        traces,
        channel_gain[None, :],
        bin_owner.reshape(1, trace_count),
        bin_slot[None, :],
        offset_class[None, :],
        shot_filter,
    )

    taps, time_taps = dip_filter.shape
    before = 192 + time_taps // 2 - (time_taps - 1)
    dip_rows = jnp.pad(
        dip_filter[:, ::-1].astype(jnp.float32),
        ((0, 0), (before, 256 - before - time_taps)),
    )
    weights = jnp.transpose(nmo_weights, (1, 0, 2)).astype(jnp.float32)
    crosslines = 2 * XL_DEV

    rim = jax.ShapeDtypeStruct((IL_DEV, half, offsets, span), jnp.bfloat16)
    sides = []
    for part in range(parts):
        rows = outgoing[part].reshape(owners, capacity, span)
        if part == 0:
            arrived, codes = exchange([rows, codes], 1)
        else:
            (arrived,) = exchange([rows], 1 + part)
        lo, hi = pl.pallas_call(
            functools.partial(bin_kernel, capacity, cells_here),
            out_shape=(rim, rim),
            in_specs=[vmem] * 2,
            out_specs=(vmem, vmem),
            compiler_params=params,
            name=f"bin_{part}",
        )(arrived.reshape(slots, span), codes)
        right = lax.ppermute(lo, "bin", [(i + 1, i) for i in range(bins - 1)])
        left = lax.ppermute(hi, "bin", [(i, i + 1) for i in range(bins - 1)])
        sides.append((left, lo, hi, right))

    per_part = span // 128
    total = samples // 128
    stacked = None
    for part in range(parts):
        first = max(per_part * part - 1, 0)
        last = per_part * (part + 1) - 1 if part < parts - 1 else total
        blocks = last - first
        low = first - 1
        operands, halves = [], []
        for piece in range(parts):
            begin = max(low, per_part * piece)
            end = min(last + 1, per_part * (piece + 1))
            if begin < end and piece <= part:
                operands += sides[piece]
                halves.append(
                    (128 * (begin - per_part * piece), 128 * (begin - low), 128 * (end - begin))
                )
        stacked = pl.pallas_call(
            functools.partial(stack_kernel, taps, first, halves),
            out_shape=jax.ShapeDtypeStruct((IL_DEV, XL_DEV, 128 * last), jnp.float32),
            in_specs=[anywhere] * len(operands) + [vmem] * (4 if first else 3),
            out_specs=vmem,
            scratch_shapes=[
                pltpu.VMEM((IL_DEV, crosslines, offsets, 128 * (blocks + 2)), jnp.bfloat16),
                pltpu.VMEM(((taps + 1) * 256, 256), jnp.bfloat16),
                pltpu.VMEM((3, IL_DEV, XL_DEV // 2, 2, offsets, 128), jnp.float32),
                pltpu.VMEM((IL_DEV, XL_DEV // 2, 2, offsets, 128), jnp.float32),
                pltpu.SemaphoreType.DMA((4 * len(halves),)),
            ],
            compiler_params=params,
            name=f"stack_{part}",
        )(*operands, *([stacked] if first else []), dip_rows, nmo_start, weights)
    return stacked


def solution(mesh):
    placed = (
        P(AXES, None),
        P(AXES, None),
        P(),
        P(AXES, None),
        P(AXES),
        P(AXES),
        P(),
        P(),
        P(),
    )
    return jax.shard_map(
        per_device, mesh=mesh, in_specs=placed, out_specs=P("shot", "bin", None), check_vma=False
    )
```

```python
import functools
import math

import jax
import jax.numpy as jnp
from jax import lax
from jax.experimental import pallas as pl
from jax.experimental.pallas import tpu as pltpu
from jax.sharding import PartitionSpec as P

IL_DEV = 2
XL_DEV = 8
MESH = pl.DeviceIdType.MESH
AXES = ("shot", "bin")
VMEM_BYTES = 40 * 1024 * 1024


def iota(shape, dim):
    return lax.broadcasted_iota(jnp.int32, shape, dim)


def toeplitz(row):
    return pltpu.roll(jnp.broadcast_to(row, (256, 256)), 0, 1, stride=1, stride_axis=0)


def decon_kernel(owners, capacity, offsets, shots, traces, table, *rest):
    outs, (codes, dec) = rest[:-2], rest[-2:]
    trace_count, samples = traces.shape
    channels = trace_count // shots
    owner_row, slot_row, class_row = (
        table[row : row + 1, :trace_count].astype(jnp.int32) for row in range(3)
    )
    hit = iota((owners, trace_count), 0) == owner_row
    hit_f = jnp.where(hit, 1.0, 0.0)
    upper = iota((trace_count, trace_count), 0) <= iota((trace_count, trace_count), 1)
    running = jnp.dot(
        hit_f.astype(jnp.bfloat16),
        jnp.where(upper, 1.0, 0.0).astype(jnp.bfloat16),
        preferred_element_type=jnp.float32,
    )
    rank = jnp.sum(jnp.where(hit, running - 1.0, 0.0), axis=0, keepdims=True)
    position = owner_row * capacity + rank.astype(jnp.int32)
    ranked = jnp.where(iota((128, trace_count), 0) == rank.astype(jnp.int32), 1.0, 0.0)
    ranked = ranked.astype(jnp.bfloat16)

    def listed(row):
        named = jnp.where(hit, row.astype(jnp.float32), 0.0).astype(jnp.bfloat16)
        return lax.dot_general(
            named, ranked, (((1,), (1,)), ((), ())), preferred_element_type=jnp.float32
        )

    bin_part = listed(slot_row + 1)
    codes[:, 0, :] = jnp.where(
        bin_part > 0, (bin_part - 1) * offsets + listed(class_row) + 1, 0.0
    )
    slots = owners * capacity
    pick = jnp.where(iota((slots, trace_count), 0) == position, 1.0, 0.0).astype(jnp.bfloat16)
    factor = jnp.broadcast_to(table[3:4, :channels], (128, channels)).T
    for shot in range(shots):
        matrix = toeplitz(table[4 + shot : 5 + shot, :256])[:, :128]
        matrix = matrix.astype(jnp.bfloat16)
        rows = slice(shot * channels, (shot + 1) * channels)
        for block in range(samples // 128):
            lanes = slice(128 * block, 128 * block + 128)
            if block == 0:
                product = jnp.dot(
                    traces[rows, lanes], matrix[128:], preferred_element_type=jnp.float32
                )
            else:
                window = slice(128 * block - 128, 128 * block + 128)
                product = jnp.dot(
                    traces[rows, window], matrix, preferred_element_type=jnp.float32
                )
            dec[rows, lanes] = (product * factor).astype(jnp.bfloat16)
    span = samples // len(outs)
    for part, out in enumerate(outs):
        for lane in range(0, span, 256):
            place = part * span + lane
            out[:, lane : lane + 256] = jnp.dot(
                pick, dec[:, place : place + 256], preferred_element_type=jnp.float32
            ).astype(jnp.bfloat16)


def exchange_kernel(shots, bins, arrays, halo, prepare, *refs):
    count = shots * bins
    refs = list(refs)

    def take(number):
        taken = refs[:number]
        del refs[:number]
        return taken

    sources = take(arrays)
    tables = take(2) if prepare else None
    lo, hi = take(2) if halo else (None, None)
    targets = take(arrays)
    results = take(2) if prepare else None
    left, right = take(2) if halo else (None, None)
    send_sems, recv_sems = take(arrays), take(arrays)
    own_sem, halo_sem = refs
    here, bin_here = lax.axis_index("shot"), lax.axis_index("bin")
    me = here * bins + bin_here
    barrier = pltpu.get_barrier_semaphore()

    def greet(step, carry):
        other = lax.rem(me + step, count)
        pl.semaphore_signal(
            barrier, inc=1, device_id=(other // bins, lax.rem(other, bins)), device_id_type=MESH
        )
        return carry

    lax.fori_loop(1, count, greet, 0)
    own = [
        pltpu.make_async_copy(sources[k].at[me], targets[k].at[me], own_sem.at[k])
        for k in range(arrays)
    ]
    for copy in own:
        copy.start()
    pl.semaphore_wait(barrier, count - 1)

    def copies_of(shot_step, bin_step):
        shot = lax.rem(here + shot_step, shots)
        crossline = lax.rem(bin_here + bin_step, bins)
        other = shot * bins + crossline
        return [
            pltpu.make_async_remote_copy(
                src_ref=sources[k].at[other],
                dst_ref=targets[k].at[me],
                send_sem=send_sems[k].at[shot_step * bins + bin_step],
                recv_sem=recv_sems[k].at[shot_step * bins + bin_step],
                device_id=(shot, crossline),
                device_id_type=MESH,
            )
            for k in range(arrays)
        ]

    far_first = sorted(range(1, shots), key=lambda step: -min(step, shots - step))

    def each(action):
        def one(bin_step, carry):
            for shot_step in far_first:
                for copy in copies_of(shot_step, bin_step):
                    action(copy)

            @pl.when(bin_step > 0)
            def _():
                for copy in copies_of(0, bin_step):
                    action(copy)

            return carry

        return one

    def rim_copy(source, target, sem, step):
        return pltpu.make_async_remote_copy(
            src_ref=source,
            dst_ref=target,
            send_sem=halo_sem.at[sem],
            recv_sem=halo_sem.at[sem + 1],
            device_id=(here, bin_here + step),
            device_id_type=MESH,
        )

    begin = each(lambda copy: copy.start())
    lax.fori_loop(0, bins // 2, begin, 0)
    if halo:

        @pl.when(bin_here < bins - 1)
        def _():
            rim_copy(hi, left, 0, 1).start()

        @pl.when(bin_here > 0)
        def _():
            rim_copy(lo, right, 2, -1).start()

    lax.fori_loop(bins // 2, bins, begin, 0)
    if prepare:
        dip_rows, nmo_weights = tables
        matrix, weights = results
        dip_matrix(dip_rows, matrix)

        def turn(block, carry):
            lanes = pl.ds(pl.multiple_of(128 * block, 128), 128)
            weights[:, :, lanes] = jnp.transpose(
                nmo_weights[:, :, lanes].astype(jnp.float32), (1, 0, 2)
            )
            return carry

        lax.fori_loop(0, nmo_weights.shape[2] // 128, turn, 0)
    if halo:

        @pl.when(bin_here == 0)
        def _():
            left[...] = jnp.zeros(left.shape, left.dtype)

        @pl.when(bin_here == bins - 1)
        def _():
            right[...] = jnp.zeros(right.shape, right.dtype)

    for copy in own:
        copy.wait()
    lax.fori_loop(0, bins, each(lambda copy: copy.wait()), 0)
    if halo:

        @pl.when(bin_here < bins - 1)
        def _():
            rim_copy(hi, left, 0, 1).wait_send()
            rim_copy(lo, right, 2, 1).wait_recv()

        @pl.when(bin_here > 0)
        def _():
            rim_copy(lo, right, 2, -1).wait_send()
            rim_copy(hi, left, 0, -1).wait_recv()


def dip_matrix(dip_rows, matrix):
    taps = dip_rows.shape[0]
    matrix[:256, 128:] = jnp.zeros((256, 128), jnp.bfloat16)
    matrix[256 * taps :, :128] = jnp.zeros((256, 128), jnp.bfloat16)
    for tap in range(taps):
        one = toeplitz(dip_rows[tap : tap + 1, :])[:, :128].astype(jnp.bfloat16)
        matrix[256 * tap : 256 * tap + 256, :128] = one
        matrix[256 * tap + 256 : 256 * tap + 512, 128:] = one


def exchange(arrays, collective_id, halo=(), tables=()):
    shots, bins = lax.axis_size("shot"), lax.axis_size("bin")
    count = shots * bins
    number = len(arrays)
    shapes = [jax.ShapeDtypeStruct(array.shape, array.dtype) for array in arrays]
    if tables:
        dip_rows, nmo_weights = tables
        offsets, taps, samples = nmo_weights.shape
        shapes.append(jax.ShapeDtypeStruct(((dip_rows.shape[0] + 1) * 256, 256), jnp.bfloat16))
        shapes.append(jax.ShapeDtypeStruct((taps, offsets, samples), jnp.float32))
    shapes += [jax.ShapeDtypeStruct(array.shape, array.dtype) for array in halo]
    operands = [*arrays, *tables, *halo]
    vmem = pl.BlockSpec(memory_space=pltpu.VMEM)
    return pl.pallas_call(
        functools.partial(exchange_kernel, shots, bins, number, bool(halo), bool(tables)),
        out_shape=shapes,
        in_specs=[vmem] * len(operands),
        out_specs=[vmem] * len(shapes),
        scratch_shapes=[pltpu.SemaphoreType.DMA((count,)) for _ in range(2 * number)]
        + [pltpu.SemaphoreType.DMA((number,)), pltpu.SemaphoreType.DMA((4,))],
        compiler_params=pltpu.CompilerParams(
            collective_id=collective_id, has_side_effects=True, vmem_limit_bytes=VMEM_BYTES
        ),
        name=f"exchange_{collective_id}",
    )(*operands)


def bin_kernel(capacity, cells_here, arrived, codes, lo, hi):
    owners = codes.shape[0]
    slots, samples = arrived.shape
    listed = codes[:, 0, :]
    place = iota((owners, slots), 1) - capacity * iota((owners, slots), 0)
    spread = jnp.zeros((owners, slots), jnp.float32)
    for rank in range(capacity):
        spread = jnp.where(place == rank, listed[:, rank : rank + 1], spread)
    slot_code = jnp.sum(spread, axis=0, keepdims=True).astype(jnp.int32)
    member_f = jnp.where(iota((cells_here, slots), 0) + 1 == slot_code, 1.0, 0.0)
    fold = jnp.sum(member_f, axis=1, keepdims=True)
    scale = 1.0 / jnp.maximum(fold, 1.0)
    member = member_f.astype(jnp.bfloat16)
    offsets = lo.shape[2]
    half = XL_DEV // 2
    for lane in range(0, samples, 256):
        summed = jnp.dot(
            member, arrived[:, lane : lane + 256], preferred_element_type=jnp.float32
        )
        binned = (summed * scale).astype(jnp.bfloat16).reshape(IL_DEV, XL_DEV, offsets, 256)
        lo[:, :, :, lane : lane + 256] = binned[:, :half]
        hi[:, :, :, lane : lane + 256] = binned[:, half:]


def stack_kernel(taps, first_block, halves, *refs):
    inputs = refs[: 4 * len(halves)]
    rest = refs[4 * len(halves) :]
    earlier = rest[0] if first_block else None
    matrix, start, weights, out, ext, ring, staged, sems = rest[1 if first_block else 0 :]
    crosslines, offsets = ext.shape[1], ext.shape[2]
    blocks = ext.shape[3] // 128 - 2
    half = crosslines // 4
    pairs = XL_DEV // 2
    copies = []
    for number, (source_lane, target_lane, span) in enumerate(halves):
        for part in range(4):
            copy = pltpu.make_async_copy(
                inputs[4 * number + part].at[:, :, :, source_lane : source_lane + span],
                ext.at[:, part * half : part * half + half, :, target_lane : target_lane + span],
                sems.at[4 * number + part],
            )
            copy.start()
            copies.append(copy)
    filled_from = min(target for _, target, _ in halves)
    filled_to = max(target + span for _, target, span in halves)
    for low, high in ((0, filled_from), (filled_to, ext.shape[3])):
        if high > low:
            ext[:, :, :, low:high] = jnp.zeros(
                (IL_DEV, crosslines, offsets, high - low), jnp.bfloat16
            )
    if first_block:
        out[:, :, : 128 * first_block] = earlier[...]
    for copy in copies:
        copy.wait()

    def filter_block(block, target):
        lanes = pl.ds(pl.multiple_of(128 * block, 128), 256)
        window = ext[:, :, :, lanes].reshape(IL_DEV, crosslines // 2, 2, offsets, 256)
        pieces = []
        for tap in range(taps + 1):
            piece = window[:, tap // 2 : tap // 2 + pairs, tap % 2]
            pieces.append(piece.reshape(IL_DEV * pairs * offsets, 256))
        result = jnp.dot(
            jnp.concatenate(pieces, axis=1), matrix[...], preferred_element_type=jnp.float32
        )
        rounded = result.astype(jnp.bfloat16).astype(jnp.float32)
        for side in range(2):
            target[:, :, side] = rounded[:, 128 * side : 128 * side + 128].reshape(
                IL_DEV, pairs, offsets, 128
            )

    filter_block(0, ring.at[0])
    filter_block(1, ring.at[1])
    nmo_taps = weights.shape[0]
    scale = 1.0 / math.sqrt(offsets)

    def stack_block(block, carry):
        filter_block(jnp.minimum(block + 2, blocks), staged)
        this, following = lax.rem(block, 3), lax.rem(block + 1, 3)
        lanes = pl.ds(pl.multiple_of(128 * (block + first_block), 128), 128)
        totals = [jnp.zeros((8, 128), jnp.float32) for _ in range(IL_DEV * XL_DEV)]
        for first in range(0, offsets, 8):
            group = slice(first, first + 8)
            at = start[group, lanes] - (128 * (block + first_block) - 64)
            for tap in range(nmo_taps):
                moved = at + tap
                index = moved & 127
                early = moved < 128
                weight = weights[tap, group, lanes]
                for cell in range(IL_DEV * XL_DEV):
                    place = (cell // XL_DEV, cell % XL_DEV // 2, cell % 2)
                    here = ring[(this,) + place + (group, slice(None))]
                    after = ring[(following,) + place + (group, slice(None))]
                    value = jnp.where(
                        early,
                        jnp.take_along_axis(here, index, axis=1),
                        jnp.take_along_axis(after, index, axis=1),
                    )
                    totals[cell] = totals[cell] + value * weight
        for inline in range(IL_DEV):
            rows = [
                jnp.sum(totals[inline * XL_DEV + x], axis=0, keepdims=True) for x in range(XL_DEV)
            ]
            out[inline, :, lanes] = jnp.concatenate(rows, axis=0) * scale
        ring[lax.rem(block + 2, 3)] = staged[...]
        return carry

    lax.fori_loop(0, blocks, stack_block, 0)


def per_device(
    traces,
    shot_filter,
    channel_gain,
    bin_owner,
    bin_slot,
    offset_class,
    dip_filter,
    nmo_start,
    nmo_weights,
):
    bins = lax.axis_size("bin")
    owners = lax.axis_size("shot") * bins
    trace_count, samples = traces.shape
    capacity = 2 * trace_count // owners
    slots = owners * capacity
    offsets = nmo_start.shape[0]
    cells_here = IL_DEV * XL_DEV * offsets
    half = XL_DEV // 2
    vmem = pl.BlockSpec(memory_space=pltpu.VMEM)
    anywhere = pl.BlockSpec(memory_space=pl.ANY)
    params = pltpu.CompilerParams(vmem_limit_bytes=VMEM_BYTES)

    parts = 2
    span = samples // parts
    row = jax.ShapeDtypeStruct((slots, span), jnp.bfloat16)
    width = max(trace_count, 256)

    def wide(array, before=0):
        array = array.astype(jnp.float32).reshape(-1, array.shape[-1])
        return jnp.pad(array, ((0, 0), (before, width - before - array.shape[1])))

    table = jnp.concatenate(
        [
            wide(bin_owner.reshape(trace_count)),
            wide(bin_slot),
            wide(offset_class),
            wide(channel_gain),
            wide(shot_filter, 128),
        ]
    )
    *outgoing, codes = pl.pallas_call(
        functools.partial(decon_kernel, owners, capacity, offsets, shot_filter.shape[0]),
        out_shape=[row] * parts + [jax.ShapeDtypeStruct((owners, 1, 128), jnp.float32)],
        in_specs=[vmem] * 2,
        out_specs=[vmem] * (parts + 1),
        scratch_shapes=[
            pltpu.VMEM(traces.shape, jnp.bfloat16),
        ],
        compiler_params=params,
        name="decon",
    )(traces, table)

    taps, time_taps = dip_filter.shape
    before = 192 + time_taps // 2 - (time_taps - 1)
    dip_rows = jnp.pad(
        dip_filter[:, ::-1].astype(jnp.float32),
        ((0, 0), (before, 256 - before - time_taps)),
    )
    crosslines = 2 * XL_DEV

    rim = jax.ShapeDtypeStruct((IL_DEV, half, offsets, span), jnp.bfloat16)
    sides = []
    for part in range(parts):
        rows = outgoing[part].reshape(owners, capacity, span)
        if part == 0:
            arrived, codes, matrix, weights = exchange(
                [rows, codes], 1, tables=(dip_rows, nmo_weights)
            )
        else:
            arrived, left, right = exchange([rows], 1 + part, halo=(lo, hi))
            sides.append((left, lo, hi, right))
        lo, hi = pl.pallas_call(
            functools.partial(bin_kernel, capacity, cells_here),
            out_shape=(rim, rim),
            in_specs=[vmem] * 2,
            out_specs=(vmem, vmem),
            compiler_params=params,
            name=f"bin_{part}",
        )(arrived.reshape(slots, span), codes)
    right = lax.ppermute(lo, "bin", [(i + 1, i) for i in range(bins - 1)])
    left = lax.ppermute(hi, "bin", [(i, i + 1) for i in range(bins - 1)])
    sides.append((left, lo, hi, right))

    per_part = span // 128
    total = samples // 128
    stacked = None
    for part in range(parts):
        first = max(per_part * part - 1, 0)
        last = per_part * (part + 1) - 1 if part < parts - 1 else total
        blocks = last - first
        low = first - 1
        operands, halves = [], []
        for piece in range(parts):
            begin = max(low, per_part * piece)
            end = min(last + 1, per_part * (piece + 1))
            if begin < end and piece <= part:
                operands += sides[piece]
                halves.append(
                    (128 * (begin - per_part * piece), 128 * (begin - low), 128 * (end - begin))
                )
        stacked = pl.pallas_call(
            functools.partial(stack_kernel, taps, first, halves),
            out_shape=jax.ShapeDtypeStruct((IL_DEV, XL_DEV, 128 * last), jnp.float32),
            in_specs=[anywhere] * len(operands) + [vmem] * (4 if first else 3),
            out_specs=vmem,
            scratch_shapes=[
                pltpu.VMEM((IL_DEV, crosslines, offsets, 128 * (blocks + 2)), jnp.bfloat16),
                pltpu.VMEM((3, IL_DEV, XL_DEV // 2, 2, offsets, 128), jnp.float32),
                pltpu.VMEM((IL_DEV, XL_DEV // 2, 2, offsets, 128), jnp.float32),
                pltpu.SemaphoreType.DMA((4 * len(halves),)),
            ],
            compiler_params=params,
            name=f"stack_{part}",
        )(*operands, *([stacked] if first else []), matrix, nmo_start, weights)
    return stacked


def solution(mesh):
    placed = (
        P(AXES, None),
        P(AXES, None),
        P(),
        P(AXES, None),
        P(AXES),
        P(AXES),
        P(),
        P(),
        P(),
    )
    return jax.shard_map(
        per_device, mesh=mesh, in_specs=placed, out_specs=P("shot", "bin", None), check_vma=False
    )
```

```python
import functools
import math

import jax
import jax.numpy as jnp
from jax import lax
from jax.experimental import pallas as pl
from jax.experimental.pallas import tpu as pltpu
from jax.sharding import PartitionSpec as P

IL_DEV = 2
XL_DEV = 8
MESH = pl.DeviceIdType.MESH
AXES = ("shot", "bin")
VMEM_BYTES = 40 * 1024 * 1024


def iota(shape, dim):
    return lax.broadcasted_iota(jnp.int32, shape, dim)


def toeplitz(row):
    return pltpu.roll(jnp.broadcast_to(row, (256, 256)), 0, 1, stride=1, stride_axis=0)


def decon_kernel(owners, capacity, offsets, shots, traces, table, *rest):
    outs, (codes, dec) = rest[:-2], rest[-2:]
    trace_count, samples = traces.shape
    channels = trace_count // shots
    owner_row, slot_row, class_row = (
        table[row : row + 1, :trace_count].astype(jnp.int32) for row in range(3)
    )
    hit = iota((owners, trace_count), 0) == owner_row
    hit_f = jnp.where(hit, 1.0, 0.0)
    upper = iota((trace_count, trace_count), 0) <= iota((trace_count, trace_count), 1)
    running = jnp.dot(
        hit_f.astype(jnp.bfloat16),
        jnp.where(upper, 1.0, 0.0).astype(jnp.bfloat16),
        preferred_element_type=jnp.float32,
    )
    rank = jnp.sum(jnp.where(hit, running - 1.0, 0.0), axis=0, keepdims=True)
    position = owner_row * capacity + rank.astype(jnp.int32)
    ranked = jnp.where(iota((128, trace_count), 0) == rank.astype(jnp.int32), 1.0, 0.0)
    ranked = ranked.astype(jnp.bfloat16)

    def listed(row):
        named = jnp.where(hit, row.astype(jnp.float32), 0.0).astype(jnp.bfloat16)
        return lax.dot_general(
            named, ranked, (((1,), (1,)), ((), ())), preferred_element_type=jnp.float32
        )

    bin_part = listed(slot_row + 1)
    codes[:, 0, :] = jnp.where(
        bin_part > 0, (bin_part - 1) * offsets + listed(class_row) + 1, 0.0
    )
    slots = owners * capacity
    pick = jnp.where(iota((slots, trace_count), 0) == position, 1.0, 0.0).astype(jnp.bfloat16)
    factor = jnp.broadcast_to(table[3:4, :channels], (128, channels)).T
    for shot in range(shots):
        matrix = toeplitz(table[4 + shot : 5 + shot, :256])[:, :128]
        matrix = matrix.astype(jnp.bfloat16)
        rows = slice(shot * channels, (shot + 1) * channels)
        for block in range(samples // 128):
            lanes = slice(128 * block, 128 * block + 128)
            if block == 0:
                product = jnp.dot(
                    traces[rows, lanes], matrix[128:], preferred_element_type=jnp.float32
                )
            else:
                window = slice(128 * block - 128, 128 * block + 128)
                product = jnp.dot(
                    traces[rows, window], matrix, preferred_element_type=jnp.float32
                )
            dec[rows, lanes] = (product * factor).astype(jnp.bfloat16)
    span = samples // len(outs)
    for part, out in enumerate(outs):
        for lane in range(0, span, 256):
            place = part * span + lane
            out[:, lane : lane + 256] = jnp.dot(
                pick, dec[:, place : place + 256], preferred_element_type=jnp.float32
            ).astype(jnp.bfloat16)


def exchange_kernel(
    shots,
    bins,
    capacity,
    cells_here,
    rows_0,
    names,
    rows_1,
    nmo_weights,
    names_in,
    arrived_1,
    weights,
    lo,
    hi,
    left,
    right,
    arrived_0,
    send_sems,
    recv_sems,
    own_sem,
    halo_sem,
):
    count = shots * bins
    here, bin_here = lax.axis_index("shot"), lax.axis_index("bin")
    me = here * bins + bin_here
    barrier = pltpu.get_barrier_semaphore()

    def greet(step, carry):
        other = lax.rem(me + step, count)
        pl.semaphore_signal(
            barrier, inc=1, device_id=(other // bins, lax.rem(other, bins)), device_id_type=MESH
        )
        return carry

    lax.fori_loop(1, count, greet, 0)
    moved = ((names, names_in), (rows_0, arrived_0), (rows_1, arrived_1))
    own = [
        pltpu.make_async_copy(source.at[me], target.at[me], own_sem.at[k])
        for k, (source, target) in enumerate(moved)
    ]
    for copy in own:
        copy.start()
    pl.semaphore_wait(barrier, count - 1)

    def copy_of(k, shot_step, bin_step):
        source, target = moved[k]
        shot = lax.rem(here + shot_step, shots)
        crossline = lax.rem(bin_here + bin_step, bins)
        step = shot_step * bins + bin_step
        return pltpu.make_async_remote_copy(
            src_ref=source.at[shot * bins + crossline],
            dst_ref=target.at[me],
            send_sem=send_sems.at[k, step],
            recv_sem=recv_sems.at[k, step],
            device_id=(shot, crossline),
            device_id_type=MESH,
        )

    far_first = sorted(range(1, shots), key=lambda step: -min(step, shots - step))

    def each(parts, action):
        def one(bin_step, carry):
            for shot_step in far_first:
                for k in parts:
                    action(copy_of(k, shot_step, bin_step))

            @pl.when(bin_step > 0)
            def _():
                for k in parts:
                    action(copy_of(k, 0, bin_step))

            return carry

        lax.fori_loop(0, bins, one, 0)

    def rim_copy(source, target, sem, step):
        return pltpu.make_async_remote_copy(
            src_ref=source,
            dst_ref=target,
            send_sem=halo_sem.at[sem],
            recv_sem=halo_sem.at[sem + 1],
            device_id=(here, bin_here + step),
            device_id_type=MESH,
        )

    each((0, 1), lambda copy: copy.start())
    each((2,), lambda copy: copy.start())

    def turn(block, carry):
        lanes = pl.ds(pl.multiple_of(128 * block, 128), 128)
        weights[:, :, lanes] = jnp.transpose(
            nmo_weights[:, :, lanes].astype(jnp.float32), (1, 0, 2)
        )
        return carry

    lax.fori_loop(0, nmo_weights.shape[2] // 128, turn, 0)

    @pl.when(bin_here == 0)
    def _():
        left[...] = jnp.zeros(left.shape, left.dtype)

    @pl.when(bin_here == bins - 1)
    def _():
        right[...] = jnp.zeros(right.shape, right.dtype)

    own[0].wait()
    own[1].wait()
    each((0, 1), lambda copy: copy.wait())
    bin_rows(capacity, cells_here, arrived_0, names_in, lo, hi)

    @pl.when(bin_here < bins - 1)
    def _():
        rim_copy(hi, left, 0, 1).start()

    @pl.when(bin_here > 0)
    def _():
        rim_copy(lo, right, 2, -1).start()

    own[2].wait()
    each((2,), lambda copy: copy.wait())

    @pl.when(bin_here < bins - 1)
    def _():
        rim_copy(hi, left, 0, 1).wait_send()
        rim_copy(lo, right, 2, 1).wait_recv()

    @pl.when(bin_here > 0)
    def _():
        rim_copy(lo, right, 2, -1).wait_send()
        rim_copy(hi, left, 0, -1).wait_recv()


def bin_rows(capacity, cells_here, arrived, names, lo, hi):
    owners, slots_each, samples = arrived.shape
    slots = owners * slots_each
    listed = names[:, 0, :]
    place = iota((owners, slots), 1) - capacity * iota((owners, slots), 0)
    spread = jnp.zeros((owners, slots), jnp.float32)
    for rank in range(capacity):
        spread = jnp.where(place == rank, listed[:, rank : rank + 1], spread)
    slot_code = jnp.sum(spread, axis=0, keepdims=True).astype(jnp.int32)
    member_f = jnp.where(iota((cells_here, slots), 0) + 1 == slot_code, 1.0, 0.0)
    fold = jnp.sum(member_f, axis=1, keepdims=True)
    scale = 1.0 / jnp.maximum(fold, 1.0)
    member = member_f.astype(jnp.bfloat16)
    offsets = lo.shape[2]
    half = XL_DEV // 2

    def chunk(number, carry):
        lanes = pl.ds(pl.multiple_of(256 * number, 256), 256)
        rows = arrived[:, :, lanes]
        if capacity % 16:
            rows = rows.astype(jnp.float32).reshape(slots, 256).astype(jnp.bfloat16)
        summed = jnp.dot(member, rows.reshape(slots, 256), preferred_element_type=jnp.float32)
        binned = (summed * scale).astype(jnp.bfloat16).reshape(IL_DEV, XL_DEV, offsets, 256)
        lo[:, :, :, lanes] = binned[:, :half]
        hi[:, :, :, lanes] = binned[:, half:]
        return carry

    lax.fori_loop(0, samples // 256, chunk, 0)


def dip_matrix(dip_rows, matrix):
    taps = dip_rows.shape[0]
    matrix[:256, 128:] = jnp.zeros((256, 128), jnp.bfloat16)
    matrix[256 * taps :, :128] = jnp.zeros((256, 128), jnp.bfloat16)
    for tap in range(taps):
        one = toeplitz(dip_rows[tap : tap + 1, :])[:128].T.astype(jnp.bfloat16)
        matrix[256 * tap : 256 * tap + 256, :128] = one
        matrix[256 * tap + 256 : 256 * tap + 512, 128:] = one


def exchange(rows_0, names, rows_1, nmo_weights, cells_here, rim):
    shots, bins = lax.axis_size("shot"), lax.axis_size("bin")
    count = shots * bins
    offsets, taps, samples = nmo_weights.shape

    def like(array):
        return jax.ShapeDtypeStruct(array.shape, array.dtype)

    vmem = pl.BlockSpec(memory_space=pltpu.VMEM)
    return pl.pallas_call(
        functools.partial(exchange_kernel, shots, bins, rows_0.shape[1], cells_here),
        out_shape=[
            like(names),
            like(rows_1),
            jax.ShapeDtypeStruct((taps, offsets, samples), jnp.float32),
        ]
        + [rim] * 4,
        in_specs=[vmem] * 4,
        out_specs=[vmem] * 7,
        scratch_shapes=[
            pltpu.VMEM(rows_0.shape, rows_0.dtype),
            pltpu.SemaphoreType.DMA((3, count)),
            pltpu.SemaphoreType.DMA((3, count)),
            pltpu.SemaphoreType.DMA((3,)),
            pltpu.SemaphoreType.DMA((4,)),
        ],
        compiler_params=pltpu.CompilerParams(
            collective_id=1, has_side_effects=True, vmem_limit_bytes=VMEM_BYTES
        ),
        name="exchange",
    )(rows_0, names, rows_1, nmo_weights)


def stack_kernel(taps, first_block, dip_row, halves, *refs):
    inputs = refs[: 4 * len(halves)]
    rest = refs[4 * len(halves) :]
    if first_block:
        earlier, matrix, start, weights, out, ext, ring, staged, sems = rest
    else:
        table, start, weights, out, matrix, ext, ring, staged, sems = rest
    crosslines, offsets = ext.shape[1], ext.shape[2]
    blocks = ext.shape[3] // 128 - 2
    half = crosslines // 4
    pairs = XL_DEV // 2
    copies = []
    for number, (source_lane, target_lane, span) in enumerate(halves):
        for part in range(4):
            copy = pltpu.make_async_copy(
                inputs[4 * number + part].at[:, :, :, source_lane : source_lane + span],
                ext.at[:, part * half : part * half + half, :, target_lane : target_lane + span],
                sems.at[4 * number + part],
            )
            copy.start()
            copies.append(copy)
    filled_from = min(target for _, target, _ in halves)
    filled_to = max(target + span for _, target, span in halves)
    for low, high in ((0, filled_from), (filled_to, ext.shape[3])):
        if high > low:
            ext[:, :, :, low:high] = jnp.zeros(
                (IL_DEV, crosslines, offsets, high - low), jnp.bfloat16
            )
    if not first_block:
        dip_matrix(table[dip_row : dip_row + taps, :256], matrix)
    else:
        out[:, :, : 128 * first_block] = earlier[...]
    for copy in copies:
        copy.wait()

    def filter_block(block, target):
        lanes = pl.ds(pl.multiple_of(128 * block, 128), 256)
        window = ext[:, :, :, lanes].reshape(IL_DEV, crosslines // 2, 2, offsets, 256)
        pieces = []
        for tap in range(taps + 1):
            piece = window[:, tap // 2 : tap // 2 + pairs, tap % 2]
            pieces.append(piece.reshape(IL_DEV * pairs * offsets, 256))
        result = jnp.dot(
            jnp.concatenate(pieces, axis=1), matrix[...], preferred_element_type=jnp.float32
        )
        rounded = result.astype(jnp.bfloat16).astype(jnp.float32)
        for side in range(2):
            target[:, :, side] = rounded[:, 128 * side : 128 * side + 128].reshape(
                IL_DEV, pairs, offsets, 128
            )

    filter_block(0, ring.at[0])
    filter_block(1, ring.at[1])
    nmo_taps = weights.shape[0]
    scale = 1.0 / math.sqrt(offsets)

    def stack_block(block, carry):
        filter_block(jnp.minimum(block + 2, blocks), staged)
        this, following = lax.rem(block, 3), lax.rem(block + 1, 3)
        lanes = pl.ds(pl.multiple_of(128 * (block + first_block), 128), 128)
        totals = [jnp.zeros((8, 128), jnp.float32) for _ in range(IL_DEV * XL_DEV)]
        for first in range(0, offsets, 8):
            group = slice(first, first + 8)
            at = start[group, lanes] - (128 * (block + first_block) - 64)
            for tap in range(nmo_taps):
                moved = at + tap
                index = moved & 127
                early = moved < 128
                weight = weights[tap, group, lanes]
                for cell in range(IL_DEV * XL_DEV):
                    place = (cell // XL_DEV, cell % XL_DEV // 2, cell % 2)
                    here = ring[(this,) + place + (group, slice(None))]
                    after = ring[(following,) + place + (group, slice(None))]
                    value = jnp.where(
                        early,
                        jnp.take_along_axis(here, index, axis=1),
                        jnp.take_along_axis(after, index, axis=1),
                    )
                    totals[cell] = totals[cell] + value * weight
        for inline in range(IL_DEV):
            rows = [
                jnp.sum(totals[inline * XL_DEV + x], axis=0, keepdims=True) for x in range(XL_DEV)
            ]
            out[inline, :, lanes] = jnp.concatenate(rows, axis=0) * scale
        ring[lax.rem(block + 2, 3)] = staged[...]
        return carry

    lax.fori_loop(0, blocks, stack_block, 0)


def per_device(
    traces,
    shot_filter,
    channel_gain,
    bin_owner,
    bin_slot,
    offset_class,
    dip_filter,
    nmo_start,
    nmo_weights,
):
    bins = lax.axis_size("bin")
    owners = lax.axis_size("shot") * bins
    trace_count, samples = traces.shape
    capacity = 2 * trace_count // owners
    slots = owners * capacity
    offsets = nmo_start.shape[0]
    cells_here = IL_DEV * XL_DEV * offsets
    half = XL_DEV // 2
    vmem = pl.BlockSpec(memory_space=pltpu.VMEM)
    anywhere = pl.BlockSpec(memory_space=pl.ANY)
    params = pltpu.CompilerParams(vmem_limit_bytes=VMEM_BYTES)

    parts = 2
    span = samples // parts
    row = jax.ShapeDtypeStruct((slots, span), jnp.bfloat16)
    width = max(trace_count, 256)

    taps, time_taps = dip_filter.shape
    shots_here = shot_filter.shape[0]
    dip_row = 4 + shots_here
    height = dip_row + taps
    lines = iota((height, width), 0)

    def one_row(array, row):
        array = array.reshape(1, -1)
        array = jnp.pad(array, ((0, 0), (0, width - array.shape[1])))
        return jnp.where(lines == row, array, jnp.zeros((), array.dtype))

    def some_rows(array, row, before):
        below = height - row - array.shape[0]
        after = width - before - array.shape[1]
        return jnp.pad(array.astype(jnp.float32), ((row, below), (before, after)))

    table = (
        (one_row(bin_owner, 0) + one_row(bin_slot, 1) + one_row(offset_class, 2)).astype(
            jnp.float32
        )
        + one_row(channel_gain, 3)
        + some_rows(shot_filter, 4, 128)
        + some_rows(dip_filter, dip_row, 64 - time_taps // 2)
    )
    *outgoing, codes = pl.pallas_call(
        functools.partial(decon_kernel, owners, capacity, offsets, shot_filter.shape[0]),
        out_shape=[row] * parts + [jax.ShapeDtypeStruct((owners, 1, 128), jnp.float32)],
        in_specs=[vmem] * 2,
        out_specs=[vmem] * (parts + 1),
        scratch_shapes=[
            pltpu.VMEM(traces.shape, jnp.bfloat16),
        ],
        compiler_params=params,
        name="decon",
    )(traces, table)

    crosslines = 2 * XL_DEV
    rim = jax.ShapeDtypeStruct((IL_DEV, half, offsets, span), jnp.bfloat16)
    rows_0, rows_1 = (rows.reshape(owners, capacity, span) for rows in outgoing)
    codes, arrived, weights, lo, hi, left, right = exchange(
        rows_0, codes, rows_1, nmo_weights, cells_here, rim
    )
    sides = [(left, lo, hi, right)]
    lo, hi = pl.pallas_call(
        functools.partial(bin_rows, capacity, cells_here),
        out_shape=(rim, rim),
        in_specs=[vmem] * 2,
        out_specs=(vmem, vmem),
        compiler_params=params,
        name="bin",
    )(arrived, codes)
    right = lax.ppermute(lo, "bin", [(i + 1, i) for i in range(bins - 1)])
    left = lax.ppermute(hi, "bin", [(i, i + 1) for i in range(bins - 1)])
    sides.append((left, lo, hi, right))

    per_part = span // 128
    total = samples // 128
    stacked = None
    for part in range(parts):
        first = max(per_part * part - 1, 0)
        last = per_part * (part + 1) - 1 if part < parts - 1 else total
        blocks = last - first
        low = first - 1
        operands, halves = [], []
        for piece in range(parts):
            begin = max(low, per_part * piece)
            end = min(last + 1, per_part * (piece + 1))
            if begin < end and piece <= part:
                operands += sides[piece]
                halves.append(
                    (128 * (begin - per_part * piece), 128 * (begin - low), 128 * (end - begin))
                )
        result = jax.ShapeDtypeStruct((IL_DEV, XL_DEV, 128 * last), jnp.float32)
        bands = jax.ShapeDtypeStruct(((taps + 1) * 256, 256), jnp.bfloat16)
        extra = (stacked, matrix) if first else (table,)
        made = pl.pallas_call(
            functools.partial(stack_kernel, taps, first, dip_row, halves),
            out_shape=[result] if first else [result, bands],
            in_specs=[anywhere] * len(operands) + [vmem] * (len(extra) + 2),
            out_specs=[vmem] * (1 if first else 2),
            scratch_shapes=[
                pltpu.VMEM((IL_DEV, crosslines, offsets, 128 * (blocks + 2)), jnp.bfloat16),
                pltpu.VMEM((3, IL_DEV, XL_DEV // 2, 2, offsets, 128), jnp.float32),
                pltpu.VMEM((IL_DEV, XL_DEV // 2, 2, offsets, 128), jnp.float32),
                pltpu.SemaphoreType.DMA((4 * len(halves),)),
            ],
            compiler_params=params,
            name=f"stack_{part}",
        )(*operands, *extra, nmo_start, weights)
        stacked = made[0]
        if not first:
            matrix = made[1]
    return stacked


def solution(mesh):
    placed = (
        P(AXES, None),
        P(AXES, None),
        P(),
        P(AXES, None),
        P(AXES),
        P(AXES),
        P(),
        P(),
        P(),
    )
    return jax.shard_map(
        per_device, mesh=mesh, in_specs=placed, out_specs=P("shot", "bin", None), check_vma=False
    )
```

```python
import functools
import math

import jax
import jax.numpy as jnp
from jax import lax
from jax.experimental import pallas as pl
from jax.experimental.pallas import tpu as pltpu
from jax.sharding import PartitionSpec as P

IL_DEV = 2
XL_DEV = 8
MESH = pl.DeviceIdType.MESH
AXES = ("shot", "bin")
VMEM_BYTES = 40 * 1024 * 1024


def iota(shape, dim):
    return lax.broadcasted_iota(jnp.int32, shape, dim)


def toeplitz(row):
    return pltpu.roll(jnp.broadcast_to(row, (256, 256)), 0, 1, stride=1, stride_axis=0)


def decon_kernel(owners, capacity, offsets, shots, traces, table, *rest):
    outs, (codes, dec) = rest[:-2], rest[-2:]
    trace_count, samples = traces.shape
    channels = trace_count // shots
    owner_row, slot_row, class_row = (
        table[row : row + 1, :trace_count].astype(jnp.int32) for row in range(3)
    )
    hit = iota((owners, trace_count), 0) == owner_row
    hit_f = jnp.where(hit, 1.0, 0.0)
    upper = iota((trace_count, trace_count), 0) <= iota((trace_count, trace_count), 1)
    running = jnp.dot(
        hit_f.astype(jnp.bfloat16),
        jnp.where(upper, 1.0, 0.0).astype(jnp.bfloat16),
        preferred_element_type=jnp.float32,
    )
    rank = jnp.sum(jnp.where(hit, running - 1.0, 0.0), axis=0, keepdims=True)
    position = owner_row * capacity + rank.astype(jnp.int32)
    ranked = jnp.where(iota((128, trace_count), 0) == rank.astype(jnp.int32), 1.0, 0.0)
    ranked = ranked.astype(jnp.bfloat16)

    def listed(row):
        named = jnp.where(hit, row.astype(jnp.float32), 0.0).astype(jnp.bfloat16)
        return lax.dot_general(
            named, ranked, (((1,), (1,)), ((), ())), preferred_element_type=jnp.float32
        )

    bin_part = listed(slot_row + 1)
    codes[:, 0, :] = jnp.where(
        bin_part > 0, (bin_part - 1) * offsets + listed(class_row) + 1, 0.0
    )
    slots = owners * capacity
    pick = jnp.where(iota((slots, trace_count), 0) == position, 1.0, 0.0).astype(jnp.bfloat16)
    factor = jnp.broadcast_to(table[3:4, :channels], (128, channels)).T
    for shot in range(shots):
        matrix = toeplitz(table[4 + shot : 5 + shot, :256])[:, :128]
        matrix = matrix.astype(jnp.bfloat16)
        rows = slice(shot * channels, (shot + 1) * channels)
        for block in range(samples // 128):
            lanes = slice(128 * block, 128 * block + 128)
            if block == 0:
                product = jnp.dot(
                    traces[rows, lanes], matrix[128:], preferred_element_type=jnp.float32
                )
            else:
                window = slice(128 * block - 128, 128 * block + 128)
                product = jnp.dot(
                    traces[rows, window], matrix, preferred_element_type=jnp.float32
                )
            dec[rows, lanes] = (product * factor).astype(jnp.bfloat16)
    first = 0
    for out in outs:
        for lane in range(0, out.shape[1], 256):
            place = first + lane
            out[:, lane : lane + 256] = jnp.dot(
                pick, dec[:, place : place + 256], preferred_element_type=jnp.float32
            ).astype(jnp.bfloat16)
        first += out.shape[1]


def exchange_kernel(
    shots,
    bins,
    capacity,
    cells_here,
    rows_0,
    names,
    rows_1,
    nmo_weights,
    weights,
    lo_0,
    hi_0,
    left_0,
    right_0,
    lo_1,
    hi_1,
    left_1,
    right_1,
    names_in,
    arrived_0,
    arrived_1,
    send_sems,
    recv_sems,
    own_sem,
    halo_sem,
):
    count = shots * bins
    here, bin_here = lax.axis_index("shot"), lax.axis_index("bin")
    me = here * bins + bin_here
    barrier = pltpu.get_barrier_semaphore()

    def greet(step, carry):
        other = lax.rem(me + step, count)
        pl.semaphore_signal(
            barrier, inc=1, device_id=(other // bins, lax.rem(other, bins)), device_id_type=MESH
        )
        return carry

    lax.fori_loop(1, count, greet, 0)
    moved = ((names, names_in), (rows_0, arrived_0), (rows_1, arrived_1))
    own = [
        pltpu.make_async_copy(source.at[me], target.at[me], own_sem.at[k])
        for k, (source, target) in enumerate(moved)
    ]
    for copy in own:
        copy.start()
    pl.semaphore_wait(barrier, count - 1)

    def copy_of(k, shot_step, bin_step):
        source, target = moved[k]
        shot = lax.rem(here + shot_step, shots)
        crossline = lax.rem(bin_here + bin_step, bins)
        step = shot_step * bins + bin_step
        return pltpu.make_async_remote_copy(
            src_ref=source.at[shot * bins + crossline],
            dst_ref=target.at[me],
            send_sem=send_sems.at[k, step],
            recv_sem=recv_sems.at[k, step],
            device_id=(shot, crossline),
            device_id_type=MESH,
        )

    far_first = sorted(range(1, shots), key=lambda step: -min(step, shots - step))

    def each(parts, action):
        def one(bin_step, carry):
            for shot_step in far_first:
                for k in parts:
                    action(copy_of(k, shot_step, bin_step))

            @pl.when(bin_step > 0)
            def _():
                for k in parts:
                    action(copy_of(k, 0, bin_step))

            return carry

        lax.fori_loop(0, bins, one, 0)

    def rim_copy(source, target, sem, step):
        return pltpu.make_async_remote_copy(
            src_ref=source,
            dst_ref=target,
            send_sem=halo_sem.at[sem],
            recv_sem=halo_sem.at[sem + 1],
            device_id=(here, bin_here + step),
            device_id_type=MESH,
        )

    each((0, 1), lambda copy: copy.start())
    each((2,), lambda copy: copy.start())

    def turn(block, carry):
        lanes = pl.ds(pl.multiple_of(128 * block, 128), 128)
        weights[:, :, lanes] = jnp.transpose(
            nmo_weights[:, :, lanes].astype(jnp.float32), (1, 0, 2)
        )
        return carry

    lax.fori_loop(0, nmo_weights.shape[2] // 128, turn, 0)

    @pl.when(bin_here == 0)
    def _():
        for left in (left_0, left_1):
            left[...] = jnp.zeros(left.shape, left.dtype)

    @pl.when(bin_here == bins - 1)
    def _():
        for right in (right_0, right_1):
            right[...] = jnp.zeros(right.shape, right.dtype)

    def send_rims(lo, hi, left, right, sem):
        @pl.when(bin_here < bins - 1)
        def _():
            rim_copy(hi, left, sem, 1).start()

        @pl.when(bin_here > 0)
        def _():
            rim_copy(lo, right, sem + 2, -1).start()

    def await_rims(lo, hi, left, right, sem):
        @pl.when(bin_here < bins - 1)
        def _():
            rim_copy(hi, left, sem, 1).wait_send()
            rim_copy(lo, right, sem + 2, 1).wait_recv()

        @pl.when(bin_here > 0)
        def _():
            rim_copy(lo, right, sem + 2, -1).wait_send()
            rim_copy(hi, left, sem, -1).wait_recv()

    own[0].wait()
    own[1].wait()
    each((0, 1), lambda copy: copy.wait())
    bin_rows(capacity, cells_here, arrived_0, names_in, lo_0, hi_0)
    send_rims(lo_0, hi_0, left_0, right_0, 0)
    own[2].wait()
    each((2,), lambda copy: copy.wait())
    bin_rows(capacity, cells_here, arrived_1, names_in, lo_1, hi_1)
    send_rims(lo_1, hi_1, left_1, right_1, 4)
    await_rims(lo_0, hi_0, left_0, right_0, 0)
    await_rims(lo_1, hi_1, left_1, right_1, 4)


def bin_rows(capacity, cells_here, arrived, names, lo, hi):
    owners, slots_each, samples = arrived.shape
    slots = owners * slots_each
    listed = names[:, 0, :]
    place = iota((owners, slots), 1) - capacity * iota((owners, slots), 0)
    spread = jnp.zeros((owners, slots), jnp.float32)
    for rank in range(capacity):
        spread = jnp.where(place == rank, listed[:, rank : rank + 1], spread)
    slot_code = jnp.sum(spread, axis=0, keepdims=True).astype(jnp.int32)
    member_f = jnp.where(iota((cells_here, slots), 0) + 1 == slot_code, 1.0, 0.0)
    fold = jnp.sum(member_f, axis=1, keepdims=True)
    scale = 1.0 / jnp.maximum(fold, 1.0)
    member = member_f.astype(jnp.bfloat16)
    offsets = lo.shape[2]
    half = XL_DEV // 2

    def chunk(number, carry):
        lanes = pl.ds(pl.multiple_of(256 * number, 256), 256)
        rows = arrived[:, :, lanes]
        if capacity % 16:
            rows = rows.astype(jnp.float32).reshape(slots, 256).astype(jnp.bfloat16)
        summed = jnp.dot(member, rows.reshape(slots, 256), preferred_element_type=jnp.float32)
        binned = (summed * scale).astype(jnp.bfloat16).reshape(IL_DEV, XL_DEV, offsets, 256)
        lo[:, :, :, lanes] = binned[:, :half]
        hi[:, :, :, lanes] = binned[:, half:]
        return carry

    lax.fori_loop(0, samples // 256, chunk, 0)


def dip_matrix(dip_rows, matrix):
    taps = dip_rows.shape[0]
    matrix[:256, 128:] = jnp.zeros((256, 128), jnp.bfloat16)
    matrix[256 * taps :, :128] = jnp.zeros((256, 128), jnp.bfloat16)
    for tap in range(taps):
        one = toeplitz(dip_rows[tap : tap + 1, :])[:128].T.astype(jnp.bfloat16)
        matrix[256 * tap : 256 * tap + 256, :128] = one
        matrix[256 * tap + 256 : 256 * tap + 512, 128:] = one


def exchange(rows_0, names, rows_1, nmo_weights, cells_here, rims):
    shots, bins = lax.axis_size("shot"), lax.axis_size("bin")
    count = shots * bins
    offsets, taps, samples = nmo_weights.shape

    vmem = pl.BlockSpec(memory_space=pltpu.VMEM)
    return pl.pallas_call(
        functools.partial(exchange_kernel, shots, bins, rows_0.shape[1], cells_here),
        out_shape=[jax.ShapeDtypeStruct((taps, offsets, samples), jnp.float32)]
        + [rim for rim in rims for _ in range(4)],
        in_specs=[vmem] * 4,
        out_specs=[vmem] * 9,
        scratch_shapes=[
            pltpu.VMEM(names.shape, names.dtype),
            pltpu.VMEM(rows_0.shape, rows_0.dtype),
            pltpu.VMEM(rows_1.shape, rows_1.dtype),
            pltpu.SemaphoreType.DMA((3, count)),
            pltpu.SemaphoreType.DMA((3, count)),
            pltpu.SemaphoreType.DMA((3,)),
            pltpu.SemaphoreType.DMA((8,)),
        ],
        compiler_params=pltpu.CompilerParams(
            collective_id=1, has_side_effects=True, vmem_limit_bytes=VMEM_BYTES
        ),
        name="exchange",
    )(rows_0, names, rows_1, nmo_weights)


def stack_kernel(taps, dip_row, halves, *refs):
    inputs = refs[: 4 * len(halves)]
    rest = refs[4 * len(halves) :]
    table, start, weights, out, matrix, ext, ring, staged, sems = rest
    crosslines, offsets = ext.shape[1], ext.shape[2]
    blocks = ext.shape[3] // 128 - 2
    half = crosslines // 4
    pairs = XL_DEV // 2
    copies = []
    for number, (source_lane, target_lane, span) in enumerate(halves):
        for part in range(4):
            copy = pltpu.make_async_copy(
                inputs[4 * number + part].at[:, :, :, source_lane : source_lane + span],
                ext.at[:, part * half : part * half + half, :, target_lane : target_lane + span],
                sems.at[4 * number + part],
            )
            copy.start()
            copies.append(copy)
    filled_from = min(target for _, target, _ in halves)
    filled_to = max(target + span for _, target, span in halves)
    for low, high in ((0, filled_from), (filled_to, ext.shape[3])):
        if high > low:
            ext[:, :, :, low:high] = jnp.zeros(
                (IL_DEV, crosslines, offsets, high - low), jnp.bfloat16
            )
    dip_matrix(table[dip_row : dip_row + taps, :256], matrix)
    for copy in copies:
        copy.wait()

    def filter_block(block, target):
        lanes = pl.ds(pl.multiple_of(128 * block, 128), 256)
        window = ext[:, :, :, lanes].reshape(IL_DEV, crosslines // 2, 2, offsets, 256)
        pieces = []
        for tap in range(taps + 1):
            piece = window[:, tap // 2 : tap // 2 + pairs, tap % 2]
            pieces.append(piece.reshape(IL_DEV * pairs * offsets, 256))
        result = jnp.dot(
            jnp.concatenate(pieces, axis=1), matrix[...], preferred_element_type=jnp.float32
        )
        rounded = result.astype(jnp.bfloat16).astype(jnp.float32)
        for side in range(2):
            target[:, :, side] = rounded[:, 128 * side : 128 * side + 128].reshape(
                IL_DEV, pairs, offsets, 128
            )

    filter_block(0, ring.at[0])
    filter_block(1, ring.at[1])
    nmo_taps = weights.shape[0]
    scale = 1.0 / math.sqrt(offsets)

    def stack_block(block, carry):
        filter_block(jnp.minimum(block + 2, blocks), staged)
        this, following = lax.rem(block, 3), lax.rem(block + 1, 3)
        lanes = pl.ds(pl.multiple_of(128 * block, 128), 128)
        totals = [jnp.zeros((8, 128), jnp.float32) for _ in range(IL_DEV * XL_DEV)]
        for first in range(0, offsets, 8):
            group = slice(first, first + 8)
            at = start[group, lanes] - (128 * block - 64)
            for tap in range(nmo_taps):
                moved = at + tap
                index = moved & 127
                early = moved < 128
                weight = weights[tap, group, lanes]
                for cell in range(IL_DEV * XL_DEV):
                    place = (cell // XL_DEV, cell % XL_DEV // 2, cell % 2)
                    here = ring[(this,) + place + (group, slice(None))]
                    after = ring[(following,) + place + (group, slice(None))]
                    value = jnp.where(
                        early,
                        jnp.take_along_axis(here, index, axis=1),
                        jnp.take_along_axis(after, index, axis=1),
                    )
                    totals[cell] = totals[cell] + value * weight
        for inline in range(IL_DEV):
            rows = [
                jnp.sum(totals[inline * XL_DEV + x], axis=0, keepdims=True) for x in range(XL_DEV)
            ]
            out[inline, :, lanes] = jnp.concatenate(rows, axis=0) * scale
        ring[lax.rem(block + 2, 3)] = staged[...]
        return carry

    lax.fori_loop(0, blocks, stack_block, 0)


def per_device(
    traces,
    shot_filter,
    channel_gain,
    bin_owner,
    bin_slot,
    offset_class,
    dip_filter,
    nmo_start,
    nmo_weights,
):
    bins = lax.axis_size("bin")
    owners = lax.axis_size("shot") * bins
    trace_count, samples = traces.shape
    capacity = 2 * trace_count // owners
    slots = owners * capacity
    offsets = nmo_start.shape[0]
    cells_here = IL_DEV * XL_DEV * offsets
    half = XL_DEV // 2
    vmem = pl.BlockSpec(memory_space=pltpu.VMEM)
    anywhere = pl.BlockSpec(memory_space=pl.ANY)
    params = pltpu.CompilerParams(vmem_limit_bytes=VMEM_BYTES)

    spans = (samples - samples // 1024 * 256, samples // 1024 * 256)
    rows = [jax.ShapeDtypeStruct((slots, span), jnp.bfloat16) for span in spans]
    width = max(trace_count, 256)

    taps, time_taps = dip_filter.shape
    shots_here = shot_filter.shape[0]
    dip_row = 4 + shots_here
    height = dip_row + taps
    lines = iota((height, width), 0)

    def one_row(array, row):
        array = array.reshape(1, -1)
        array = jnp.pad(array, ((0, 0), (0, width - array.shape[1])))
        return jnp.where(lines == row, array, jnp.zeros((), array.dtype))

    def some_rows(array, row, before):
        below = height - row - array.shape[0]
        after = width - before - array.shape[1]
        return jnp.pad(array.astype(jnp.float32), ((row, below), (before, after)))

    table = (
        (one_row(bin_owner, 0) + one_row(bin_slot, 1) + one_row(offset_class, 2)).astype(
            jnp.float32
        )
        + one_row(channel_gain, 3)
        + some_rows(shot_filter, 4, 128)
        + some_rows(dip_filter, dip_row, 64 - time_taps // 2)
    )
    *outgoing, codes = pl.pallas_call(
        functools.partial(decon_kernel, owners, capacity, offsets, shot_filter.shape[0]),
        out_shape=rows + [jax.ShapeDtypeStruct((owners, 1, 128), jnp.float32)],
        in_specs=[vmem] * 2,
        out_specs=[vmem] * (len(spans) + 1),
        scratch_shapes=[
            pltpu.VMEM(traces.shape, jnp.bfloat16),
        ],
        compiler_params=params,
        name="decon",
    )(traces, table)

    crosslines = 2 * XL_DEV
    rims = [
        jax.ShapeDtypeStruct((IL_DEV, half, offsets, span), jnp.bfloat16) for span in spans
    ]
    rows_0, rows_1 = (
        rows.reshape(owners, capacity, span) for rows, span in zip(outgoing, spans)
    )
    weights, lo_0, hi_0, left_0, right_0, lo_1, hi_1, left_1, right_1 = exchange(
        rows_0, codes, rows_1, nmo_weights, cells_here, rims
    )
    operands = (left_0, lo_0, hi_0, right_0, left_1, lo_1, hi_1, right_1)
    pieces = ((0, 128, spans[0]), (0, 128 + spans[0], spans[1]))
    return pl.pallas_call(
        functools.partial(stack_kernel, taps, dip_row, pieces),
        out_shape=jax.ShapeDtypeStruct((IL_DEV, XL_DEV, samples), jnp.float32),
        in_specs=[anywhere] * len(operands) + [vmem] * 3,
        out_specs=vmem,
        scratch_shapes=[
            pltpu.VMEM(((taps + 1) * 256, 256), jnp.bfloat16),
            pltpu.VMEM((IL_DEV, crosslines, offsets, samples + 256), jnp.bfloat16),
            pltpu.VMEM((3, IL_DEV, XL_DEV // 2, 2, offsets, 128), jnp.float32),
            pltpu.VMEM((IL_DEV, XL_DEV // 2, 2, offsets, 128), jnp.float32),
            pltpu.SemaphoreType.DMA((len(operands),)),
        ],
        compiler_params=params,
        name="stack",
    )(*operands, table, nmo_start, weights)


def solution(mesh):
    placed = (
        P(AXES, None),
        P(AXES, None),
        P(),
        P(AXES, None),
        P(AXES),
        P(AXES),
        P(),
        P(),
        P(),
    )
    return jax.shard_map(
        per_device, mesh=mesh, in_specs=placed, out_specs=P("shot", "bin", None), check_vma=False
    )
```
